128 devices in a mesh: row: 16 (over y, x_hi, core), col: 8 (over z, x_lo).
Axes of the slice: x: 4 (x_hi: 2, x_lo: 2; x = x_hi * 2 + x_lo), y: 4, z: 4, core: 2. Of those that a mesh axis runs over, the one named last changes fastest.
Arguments:
- homolog_embedding: bfloat16 [1024, 1024, 256], P(('row', 'col')), may hold values from -6 to 6
- presence_indicator: int32 [1024, 1024], P(('row', 'col')), may hold values 0 or 1
- standardizer_multiplier: float32 [256], replicated, may hold values from 0.5 to 1.5
- standardizer_offset: float32 [256], replicated, may hold values from -1.5 to 1.5
- first_factor_matrix: bfloat16 [256, 32], replicated, may hold values from -0.375 to 0.375
- first_factor_offset: float32 [32], replicated, may hold values from -1.5 to 1.5
- second_factor_matrix: bfloat16 [256, 32], replicated, may hold values from -0.375 to 0.375
- second_factor_offset: float32 [32], replicated, may hold values from -1.5 to 1.5
- final_matrix: bfloat16 [1024, 128], replicated, may hold values from -0.59765625 to 0.59765625
- final_offset: float32 [128], replicated, may hold values from -1.5 to 1.5
Outputs:
- pair_update: bfloat16 [1024, 1024, 128], P('row', 'col')
The draws below stay inside these ranges and needn't reach their ends.
All inputs are finite; a program needn't handle non-finite values. No bound on the sum of `presence_indicator` on one device may be relied on, other than what follows from the above.
Results may differ from the reference program's by a relative error of at most 0.0052.
Values may be sent and summed in bfloat16 or wider, within the bound.
A program may use at most 320 MiB of HBM per device.

```python
import jax
import jax.numpy as jnp
from jax import lax

EMBED_DEPTH = 256
HIDDEN_FEATURES = 32
CZ = 128
RES_ROW = 64
HOMOLOG_TOTAL = 1024
POSITION_TOTAL = 1024


def touch_ends(entries, stream_key, low, high):
    index_at = [jax.random.randint(jax.random.fold_in(stream_key, axis), (), 0, length) for axis, length in enumerate(entries.shape)]
    longest = entries.shape.index(max(entries.shape))
    neighbour = index_at[:longest] + [(index_at[longest] + 1) % entries.shape[longest]] + index_at[longest + 1:]
    return entries.at[tuple(index_at)].set(low).at[tuple(neighbour)].set(high)


def block_scale(own_key, shape, pieces, smallest, high):
    def one(dim, blocks):
        steps = jax.random.uniform(jax.random.fold_in(jax.random.fold_in(own_key, 6), dim), (blocks,), jnp.float32, smallest / len(pieces), high / len(pieces))
        return jnp.repeat(jnp.exp(steps), shape[dim] // blocks).reshape((-1,) + (1,) * (len(shape) - dim - 1))

    gain = one(*pieces[0])
    for cut in pieces[1:]:
        gain = gain * one(*cut)
    return gain


def noise(rng, dims, deviation, bound, shards=(), held_as=jnp.bfloat16):
    level = block_scale(rng, dims, shards, -0.22, 0.18) if shards else 1.0
    entries = jax.random.normal(rng, dims, jnp.float32) * deviation * level
    return jnp.minimum(jnp.maximum(entries, -bound), bound).astype(held_as)


def setup_inputs(seed: int = 0) -> dict:
    streams_of = jax.random.split(jax.random.key(seed), 11)
    return {
        "homolog_embedding": noise(streams_of[0], (HOMOLOG_TOTAL, POSITION_TOTAL, EMBED_DEPTH), 1.0, 6.0, ((0, 128),)),
        "presence_indicator": touch_ends((jax.random.randint(streams_of[1], (HOMOLOG_TOTAL, POSITION_TOTAL), 0, 4) < 3).astype(jnp.int32), jax.random.fold_in(streams_of[1], 1), 0, 1),
        "standardizer_multiplier": jnp.clip(1.0 + 0.1 * jax.random.normal(streams_of[2], (EMBED_DEPTH,), jnp.float32), 0.5, 1.5),
        "standardizer_offset": noise(streams_of[3], (EMBED_DEPTH,), 0.3, 1.5, (), jnp.float32),
        "first_factor_matrix": noise(streams_of[4], (EMBED_DEPTH, HIDDEN_FEATURES), EMBED_DEPTH ** -0.5, 0.375),
        "first_factor_offset": noise(streams_of[5], (HIDDEN_FEATURES,), 0.3, 1.5, (), jnp.float32),
        "second_factor_matrix": noise(streams_of[6], (EMBED_DEPTH, HIDDEN_FEATURES), EMBED_DEPTH ** -0.5, 0.375),
        "second_factor_offset": noise(streams_of[7], (HIDDEN_FEATURES,), 0.3, 1.5, (), jnp.float32),
        "final_matrix": noise(streams_of[8], (HIDDEN_FEATURES * HIDDEN_FEATURES, CZ), 0.1, 0.59765625),
        "final_offset": noise(streams_of[9], (CZ,), 0.3, 1.5, (), jnp.float32),
    }


def standardize_features(homolog_embedding, standardizer_multiplier, standardizer_offset):
    input_tensor = homolog_embedding.astype(jnp.float32)
    center = lax.optimization_barrier(jnp.mean(input_tensor, axis=-1, keepdims=True))
    spread = lax.optimization_barrier(jnp.mean((input_tensor - center) ** 2, axis=-1, keepdims=True))
    return ((input_tensor - center) * lax.rsqrt(spread + 1e-05) * standardizer_multiplier + standardizer_offset).astype(jnp.bfloat16)

def linear_map(standardized_embedding, numeric_indicator, coefficient_matrix, additive_offset):
    reshaped_matrix = standardized_embedding.reshape(-1, standardized_embedding.shape[-1])
    input_tensor = jnp.dot(reshaped_matrix, coefficient_matrix, preferred_element_type=jnp.float32).reshape(standardized_embedding.shape[:-1] + (coefficient_matrix.shape[1],))
    return (numeric_indicator[..., None] * (input_tensor + additive_offset)).astype(jnp.bfloat16)

def reference(homolog_embedding, presence_indicator, standardizer_multiplier, standardizer_offset, first_factor_matrix, first_factor_offset, second_factor_matrix, second_factor_offset, final_matrix, final_offset):
    numeric_indicator = presence_indicator.astype(jnp.float32)
    standardized_embedding = standardize_features(homolog_embedding, standardizer_multiplier, standardizer_offset)
    first_factor = linear_map(standardized_embedding, numeric_indicator, first_factor_matrix, first_factor_offset)
    second_factor = linear_map(standardized_embedding, numeric_indicator, second_factor_matrix, second_factor_offset)
    count = jnp.dot(numeric_indicator.T, numeric_indicator, precision=lax.Precision.HIGHEST)
    width = HIDDEN_FEATURES
    blocks = POSITION_TOTAL // RES_ROW
    right_flat = second_factor.reshape(HOMOLOG_TOTAL, POSITION_TOTAL * width).astype(jnp.float32)
    left_blocks = first_factor.reshape(HOMOLOG_TOTAL, blocks, RES_ROW, width).transpose(1, 0, 2, 3)
    count_blocks = count.reshape(blocks, RES_ROW, POSITION_TOTAL)
    weight3 = final_matrix.reshape(width, width, CZ).astype(jnp.float32)

    def one_block(item):
        left_blk, count_blk = item
        outer = jnp.einsum('sa,sb->ab', left_blk.reshape(HOMOLOG_TOTAL, RES_ROW * width).astype(jnp.float32), right_flat)
        outer = outer.reshape(RES_ROW, width, POSITION_TOTAL, width)
        mean = (outer / (count_blk[:, None, :, None] + 0.001)).astype(jnp.bfloat16)
        update = jnp.einsum('icje,ceh->ijh', mean.astype(jnp.float32), weight3) + final_offset
        return update.astype(jnp.bfloat16)
    result = lax.map(one_block, (left_blocks, count_blocks))
    return result.reshape(POSITION_TOTAL, POSITION_TOTAL, CZ)
```

```python
import jax
import jax.numpy as jnp
from jax import lax
from jax.experimental import pallas as pl
from jax.experimental.pallas import tpu as pltpu
from jax.sharding import PartitionSpec as P

F32 = jnp.float32
BF16 = jnp.bfloat16
MESH = pl.DeviceIdType.MESH

SEQS = 8
RES = 1024
CH = 256
HALF = 16
GROUPS = 4
NI = 64 // GROUPS
NE = HALF // GROUPS
PIECE = (HALF + 2) * SEQS
DEPTH = 128


def column(row, n):
    eye = lax.broadcasted_iota(jnp.int32, (n, n), 0) == lax.broadcasted_iota(jnp.int32, (n, n), 1)
    return jnp.sum(jnp.where(eye, jnp.broadcast_to(row, (n, n)), 0.0), axis=1, keepdims=True)


def kernel(
    x_hbm, m_ref, gain_ref, off_ref, w1_ref, b1_ref, w2_ref, b2_ref, ft_ref, fo_ref,
    out_hbm,
    xv, wst, cst, stage, sbuf, abuf, t2, tm, lg, ls, rg, rs, lm, rm, mid, acc, cnt, ob,
    xsem, asend, arecv, gsend, grecv, ssend, srecv, msend, mrecv, osem,
):
    row = lax.axis_index("row")
    col = lax.axis_index("col")
    core = lax.rem(row, 2)
    sibling = row + 1 - 2 * core
    own = (col, row // 2)
    place = (row, col * 2 + core)

    def exchange_id(mat, p):
        return (p, col) if mat == 0 else ((row // 2) * 2 + lax.rem(p, 2), p // 2)

    def gather_id(mat, k):
        return (row, k) if mat == 0 else (k * 2 + core, col)

    barrier = pltpu.get_barrier_semaphore()

    def hello(d, c):
        pl.semaphore_signal(barrier, inc=1, device_id=exchange_id(0, lax.rem(row + d, 16)), device_id_type=MESH)
        return c

    def hello_cols(d, c):
        k = lax.rem(col + d, 8)
        pl.semaphore_signal(barrier, inc=1, device_id=(row, k), device_id_type=MESH)
        pl.semaphore_signal(barrier, inc=1, device_id=(sibling, k), device_id_type=MESH)
        return c

    lax.fori_loop(1, 16, hello, 0)
    lax.fori_loop(1, 8, hello_cols, 0)

    def xcopy(s):
        return pltpu.make_async_copy(x_hbm.at[s], xv.at[s], xsem.at[s])

    for s in range(SEQS):
        xcopy(s).start()

    wt = jnp.concatenate([w1_ref[...].astype(F32).T, w2_ref[...].astype(F32).T], axis=0)
    gw = wt * gain_ref[...]
    hi = gw.astype(BF16)
    lo = (gw - hi.astype(F32)).astype(BF16)
    wst[0:64] = hi
    wst[64:128] = lo
    wst[128:144] = jnp.ones((16, CH), BF16)
    cst[0] = jnp.broadcast_to(jnp.sum(hi.astype(F32) + lo.astype(F32), axis=1, keepdims=True), (64, 128))
    bias = jnp.concatenate([column(b1_ref[...], 32), column(b2_ref[...], 32)], axis=0)
    cst[1] = jnp.broadcast_to(jnp.sum(wt * off_ref[...], axis=1, keepdims=True) + bias, (64, 128))

    def project(s, c):
        xcopy(s).wait()
        x = xv[s]
        p = lax.dot_general(wst[...], x, (((1,), (1,)), ((), ())), preferred_element_type=F32)
        mean_rows = jnp.dot(x, jnp.ones((CH, 128), BF16), preferred_element_type=F32) * (1.0 / CH)
        xf = x.astype(F32)
        d0 = xf[:, :128] - mean_rows
        d1 = xf[:, 128:] - mean_rows
        sq = jnp.concatenate([(d0 * d0).astype(BF16), (d1 * d1).astype(BF16)], axis=1)
        v = lax.dot_general(jnp.ones((16, CH), BF16), sq, (((1,), (1,)), ((), ())), preferred_element_type=F32)
        for t in range(8):
            lanes = slice(t * 128, (t + 1) * 128)
            mean = p[128:129, lanes] * (1.0 / CH)
            scale = lax.rsqrt(v[0:1, lanes] * (1.0 / CH) + 1e-5)
            y = (p[0:64, lanes] + p[64:128, lanes] - mean * cst[0]) * scale + cst[1]
            stage[t, pl.ds(s, 64, stride=SEQS), :] = y
        return c

    lax.fori_loop(0, SEQS, project, 0)

    for t in range(8):
        mask = m_ref[:, t * 128 : (t + 1) * 128].astype(F32)
        mask2 = jnp.concatenate([mask, mask], axis=0).astype(BF16)
        for mat in range(2):
            for h in range(2):
                at = mat * 256 + h * 128
                y = stage[t, at : at + 128, :].reshape(HALF, SEQS, 128) * mask
                sbuf[mat, t * 2 + h, 0:128, :] = y.reshape(128, 128).astype(BF16)
                sbuf[mat, t * 2 + h, 128:144, :] = mask2

    pl.semaphore_wait(barrier, 29)

    def acopy(mat, p):
        return pltpu.make_async_remote_copy(
            src_ref=sbuf.at[mat, p], dst_ref=abuf.at[mat, place[mat]],
            send_sem=asend.at[mat, p], recv_sem=arecv.at[mat, place[mat]],
            device_id=exchange_id(mat, p), device_id_type=MESH)

    def aland(mat, p):
        return pltpu.make_async_remote_copy(
            src_ref=sbuf.at[mat, p], dst_ref=abuf.at[mat, p],
            send_sem=asend.at[mat, p], recv_sem=arecv.at[mat, p],
            device_id=exchange_id(mat, p), device_id_type=MESH)

    def asend_all(d, c):
        for mat in range(2):
            acopy(mat, lax.rem(place[mat] + d, 16)).start()
        return c

    lax.fori_loop(1, 16, asend_all, 0)
    for mat in range(2):
        abuf[mat, place[mat]] = sbuf[mat, place[mat]]
    acc[...] = jnp.zeros_like(acc)

    def await_all(mat):
        def one(d, c):
            aland(mat, lax.rem(place[mat] + d, 16)).wait_recv()
            return c

        lax.fori_loop(1, 16, one, 0)

    def slot(mat, g, k):
        return lg.at[g, k] if mat == 0 else rg.at[g, :, k]

    def gcopy(mat, g, k, to, n):
        return pltpu.make_async_remote_copy(
            src_ref=slot(mat, g, k), dst_ref=slot(mat, g, k),
            send_sem=gsend.at[mat, g, n], recv_sem=grecv.at[mat, g, k],
            device_id=gather_id(mat, to), device_id_type=MESH)

    def scopy(mat, g, k):
        src = lg.at[g, k, 1] if mat == 0 else rg.at[g, :, k]
        dst = ls.at[g, k] if mat == 0 else rs.at[g, :, k]
        return pltpu.make_async_remote_copy(
            src_ref=src, dst_ref=dst,
            send_sem=ssend.at[mat, g, k], recv_sem=srecv.at[mat, g, k],
            device_id=(sibling, col), device_id_type=MESH)

    def mslot(mat, k):
        return lm.at[k] if mat == 0 else rm.at[:, k]

    def mcopy(mat, k, to):
        return pltpu.make_async_remote_copy(
            src_ref=mslot(mat, k), dst_ref=mslot(mat, k),
            send_sem=msend.at[mat, to], recv_sem=mrecv.at[mat, k],
            device_id=gather_id(mat, to), device_id_type=MESH)

    mate = tuple(k + 1 - 2 * lax.rem(k, 2) for k in own)

    def ring(k, steps):
        return lax.rem(k + 2 * steps, 8)

    def to_mate(mat, g):
        gcopy(mat, g, own[mat], mate[mat], 0).start()

    def to_ring(mat, g):
        k = own[mat]
        gcopy(mat, g, k, ring(k, 1), 1).start()
        gcopy(mat, g, k, ring(k, 3), 2).start()
        scopy(mat, g, k).start()

    def landed(mat, g, k):
        gcopy(mat, g, k, mate[mat], 0).wait_recv()

    def s1(mat, g):
        k = own[mat]
        landed(mat, g, mate[mat])
        gcopy(mat, g, mate[mat], ring(k, 1), 3).start()
        gcopy(mat, g, mate[mat], ring(k, 3), 4).start()
        scopy(mat, g, mate[mat]).start()

    def s2(mat, g):
        k = own[mat]
        landed(mat, g, ring(k, 3))
        gcopy(mat, g, ring(k, 3), ring(k, 1), 5).start()
        landed(mat, g, ring(k, 1))
        scopy(mat, g, ring(k, 3)).start()
        scopy(mat, g, ring(k, 1)).start()

    def s3(mat, g):
        k = own[mat]
        landed(mat, g, ring(mate[mat], 1))
        gcopy(mat, g, ring(mate[mat], 1), ring(k, 3), 6).start()
        landed(mat, g, ring(mate[mat], 3))
        scopy(mat, g, ring(mate[mat], 1)).start()
        scopy(mat, g, ring(mate[mat], 3)).start()

    def s4(mat, g):
        for k in (ring(own[mat], 2), ring(mate[mat], 2)):
            landed(mat, g, k)
            scopy(mat, g, k).start()

    def s5(mat, g):
        def one(k, c):
            scopy(mat, g, k).wait_recv()
            return c

        lax.fori_loop(0, 8, one, 0)

    await_all(1)
    for pair in range(HALF // 2 + 1):
        part = abuf[1, :, pair * 16 : pair * 16 + 16, :].astype(F32).reshape(16, 2, 8, 128)
        for q in range(2):
            e = pair * 2 + q
            tile = part[:, q].reshape(8, 16, 128).astype(BF16)
            if e < HALF:
                at = (e % NE) * 128
                rg[e // NE, :, own[1], :, at : at + 128] = tile
            elif e == HALF:
                rm[:, own[1]] = tile
    for g in range(2):
        to_mate(1, g)
        to_ring(1, g)

    await_all(0)
    for pair in range(HALF // 2 + 1):
        part = abuf[0, :, pair * 16 : pair * 16 + 16, :].astype(F32).reshape(16, 2, 8, 128)
        for q in range(2):
            c = pair * 2 + q
            if c <= HALF:
                tile = part[:, q].reshape(128, 128).T
                if c < HALF:
                    t2[pl.ds(c, 128, stride=HALF), :] = tile
                else:
                    tm[...] = tile
    for g in range(GROUPS):
        for rel in range(2):
            half = core if rel == 0 else 1 - core
            rows = pl.multiple_of((half * 64 + g * NI) * HALF, NI * HALF)
            lg[g, own[0], rel] = t2[pl.ds(rows, NI * HALF), :].astype(BF16)
    lm[own[0]] = tm[pl.ds(pl.multiple_of(core * 64, 64), 64), :].astype(BF16)
    for g in range(2):
        to_mate(0, g)
        to_ring(0, g)
    for mat in range(2):
        for g in range(2, GROUPS):
            to_mate(mat, g)

    def send_masks(d, c):
        for mat in range(2):
            mcopy(mat, own[mat], lax.rem(own[mat] + d, 8)).start()
        return c

    lax.fori_loop(1, 8, send_masks, 0)

    def block(gl, gr):
        for rh in range(2):
            rhs = (rg if rh == 0 else rs)[gr].reshape(1024, NE * 128)
            for lh in range(2):
                lhs = jnp.concatenate([lg[gl, k, 0] if lh == 0 else ls[gl, k] for k in range(8)], axis=1)
                o = jnp.dot(lhs, rhs, preferred_element_type=F32).astype(BF16)
                for e in range(NE):
                    at = ((rh * NE + e) * 2 + lh) * 16
                    for i in range(NI):
                        mid[at : at + 16, i * 128 : (i + 1) * 128] = o[i * 16 : (i + 1) * 16, e * 128 : (e + 1) * 128]
        acc[gl] += jnp.dot(ft_ref[gr], mid[...], preferred_element_type=F32)

    def ocopy(gl):
        return pltpu.make_async_copy(ob.at[gl], out_hbm.at[pl.ds(gl * NI, NI)], osem.at[gl])

    def finish(gl):
        offset = jnp.broadcast_to(column(fo_ref[...], DEPTH), (DEPTH, 128))

        def one(i, c):
            lanes = pl.ds(pl.multiple_of(i * 128, 128), 128)
            y = acc[gl, :, lanes] * cnt[pl.ds(gl * NI + i, 1), :] + offset
            ob[gl, i] = y.T.astype(BF16)
            return c

        lax.fori_loop(0, NI, one, 0)
        ocopy(gl).start()

    both = (0, 1)

    def serve(f, g):
        for mat in both:
            f(mat, g)

    def compute(g, last=False):
        def along_right(r, c):
            block(g, r)
            return c

        def along_left(l, c):
            block(l, g)
            if last:
                finish(l)
            return c

        lax.fori_loop(0, g + 1, along_right, 0)
        if last:
            finish(g)
        if g > 0:
            lax.fori_loop(0, g, along_left, 0)

    for f in (s1, s2, s3):
        serve(f, 0)
    serve(to_ring, 2)
    for f in (s1, s2, s3):
        serve(f, 1)
    serve(s4, 0)
    serve(s5, 0)
    compute(0)
    serve(to_ring, 3)
    for f in (s1, s2, s3):
        serve(f, 2)
    serve(s4, 1)
    serve(s5, 1)
    compute(1)
    for f in (s1, s2, s3):
        serve(f, 3)
    serve(s4, 2)
    serve(s5, 2)

    def await_masks(d, c):
        for mat in both:
            k = lax.rem(own[mat] + d, 8)
            mcopy(mat, k, k).wait_recv()
        return c

    lax.fori_loop(1, 8, await_masks, 0)
    count = jnp.dot(
        jnp.concatenate([lm[k] for k in range(8)], axis=1), rm[...].reshape(1024, 128), preferred_element_type=F32)
    cnt[...] = 1.0 / (count + 0.001)

    compute(2)
    serve(s4, 3)
    serve(s5, 3)
    compute(3, last=True)

    def asent(d, c):
        for mat in both:
            acopy(mat, lax.rem(place[mat] + d, 16)).wait_send()
        return c

    def msent(d, c):
        for mat in both:
            mcopy(mat, own[mat], lax.rem(own[mat] + d, 8)).wait_send()
        return c

    def gsent(g, c):
        for mat in both:
            for n in range(7):
                gcopy(mat, g, own[mat], mate[mat], n).wait_send()
            for k in range(8):
                scopy(mat, g, k).wait_send()
        return c

    lax.fori_loop(1, 16, asent, 0)
    lax.fori_loop(1, 8, msent, 0)
    lax.fori_loop(0, GROUPS, gsent, 0)
    for gl in range(GROUPS):
        ocopy(gl).wait()


def shards(x, mask, gain, off, w1, b1, w2, b2, final, final_offset):
    core = lax.rem(lax.axis_index("row"), 2)
    ft = final.reshape(2, HALF, 2, GROUPS, NE, DEPTH).transpose(3, 5, 2, 4, 0, 1)
    ft = jnp.where(core == 0, ft, ft[:, :, ::-1, :, ::-1, :]).reshape(GROUPS, DEPTH, 64 * NE)
    vmem = pl.BlockSpec(memory_space=pltpu.VMEM)
    hbm = pl.BlockSpec(memory_space=pl.ANY)
    dma = pltpu.SemaphoreType.DMA
    return pl.pallas_call(
        kernel,
        out_shape=jax.ShapeDtypeStruct((64, 128, DEPTH), BF16),
        in_specs=[hbm] + [vmem] * 9,
        out_specs=hbm,
        scratch_shapes=[
            pltpu.VMEM((SEQS, RES, CH), BF16),
            pltpu.VMEM((144, CH), BF16),
            pltpu.VMEM((2, 64, 128), F32),
            pltpu.VMEM((8, 64 * SEQS, 128), F32),
            pltpu.VMEM((2, 16, PIECE, 128), BF16),
            pltpu.VMEM((2, 16, PIECE, 128), BF16),
            pltpu.VMEM((128 * HALF, 128), F32),
            pltpu.VMEM((128, 128), F32),
            pltpu.VMEM((GROUPS, 8, 2, NI * HALF, 128), BF16),
            pltpu.VMEM((GROUPS, 8, NI * HALF, 128), BF16),
            pltpu.VMEM((GROUPS, 8, 8, 16, NE * 128), BF16),
            pltpu.VMEM((GROUPS, 8, 8, 16, NE * 128), BF16),
            pltpu.VMEM((8, 64, 128), BF16),
            pltpu.VMEM((8, 8, 16, 128), BF16),
            pltpu.VMEM((64 * NE, NI * 128), BF16),
            pltpu.VMEM((GROUPS, DEPTH, NI * 128), F32),
            pltpu.VMEM((64, 128), F32),
            pltpu.VMEM((GROUPS, NI, 128, DEPTH), BF16),
            dma((SEQS,)),
            dma((2, 16)),
            dma((2, 16)),
            dma((2, GROUPS, 8)),
            dma((2, GROUPS, 8)),
            dma((2, GROUPS, 8)),
            dma((2, GROUPS, 8)),
            dma((2, 8)),
            dma((2, 8)),
            dma((GROUPS,)),
        ],
        compiler_params=pltpu.CompilerParams(
            collective_id=0, has_side_effects=True, vmem_limit_bytes=56 * 1024 * 1024),
        cost_estimate=pl.CostEstimate(flops=20_000_000_000, bytes_accessed=8_000_000, transcendentals=0),
    )(x, mask, gain.reshape(1, CH), off.reshape(1, CH), w1, b1.reshape(1, 32), w2, b2.reshape(1, 32), ft,
      final_offset.reshape(1, DEPTH))


def solution(mesh):
    every = P(("row", "col"))
    in_specs = (every, every) + (P(),) * 8
    return jax.shard_map(shards, mesh=mesh, in_specs=in_specs, out_specs=P("row", "col", None), check_vma=False)
```

```python
import jax
import jax.numpy as jnp
from jax import lax
from jax.experimental import pallas as pl
from jax.experimental.pallas import tpu as pltpu
from jax.sharding import PartitionSpec as P

F32 = jnp.float32
BF16 = jnp.bfloat16
MESH = pl.DeviceIdType.MESH

SEQS = 8
RES = 1024
CH = 256
HALF = 16
GROUPS = 4
NI = 64 // GROUPS
NE = HALF // GROUPS
PIECE = (HALF + 2) * SEQS
DEPTH = 128


def column(row, n):
    eye = lax.broadcasted_iota(jnp.int32, (n, n), 0) == lax.broadcasted_iota(jnp.int32, (n, n), 1)
    return jnp.sum(jnp.where(eye, jnp.broadcast_to(row, (n, n)), 0.0), axis=1, keepdims=True)


def kernel(
    x_hbm, m_ref, gain_ref, off_ref, w1_ref, b1_ref, w2_ref, b2_ref, f_ref, fo_ref,
    out_hbm,
    xv, wst, cst, fsc, ft_ref, stage, sbuf, abuf, t2, tm, lg, ls, rg, rs, lm, rm, mid, acc, cnt, ob,
    xsem, asend, arecv, gsend, grecv, ssend, srecv, msend, mrecv, osem,
):
    row = lax.axis_index("row")
    col = lax.axis_index("col")
    core = lax.rem(row, 2)
    sibling = row + 1 - 2 * core
    own = (col, row // 2)
    place = (row, col * 2 + core)

    def exchange_id(mat, p):
        return (p, col) if mat == 0 else ((row // 2) * 2 + lax.rem(p, 2), p // 2)

    def gather_id(mat, k):
        return (row, k) if mat == 0 else (k * 2 + core, col)

    barrier = pltpu.get_barrier_semaphore()

    def hello(d, c):
        pl.semaphore_signal(barrier, inc=1, device_id=exchange_id(0, lax.rem(row + d, 16)), device_id_type=MESH)
        return c

    def hello_cols(d, c):
        k = lax.rem(col + d, 8)
        pl.semaphore_signal(barrier, inc=1, device_id=(row, k), device_id_type=MESH)
        pl.semaphore_signal(barrier, inc=1, device_id=(sibling, k), device_id_type=MESH)
        return c

    lax.fori_loop(1, 16, hello, 0)
    lax.fori_loop(1, 8, hello_cols, 0)

    def xcopy(s):
        return pltpu.make_async_copy(x_hbm.at[s], xv.at[s], xsem.at[s])

    for s in range(SEQS):
        xcopy(s).start()

    wt = jnp.concatenate([w1_ref[...].astype(F32), w2_ref[...].astype(F32)], axis=0)
    gw = wt * gain_ref[...]
    hi = gw.astype(BF16)
    lo = (gw - hi.astype(F32)).astype(BF16)
    wst[0:64] = hi
    wst[64:128] = lo
    wst[128:144] = jnp.ones((16, CH), BF16)
    cst[0] = jnp.broadcast_to(jnp.sum(hi.astype(F32) + lo.astype(F32), axis=1, keepdims=True), (64, 128))
    bias = jnp.concatenate([column(b1_ref[...], 32), column(b2_ref[...], 32)], axis=0)
    cst[1] = jnp.broadcast_to(jnp.sum(wt * off_ref[...], axis=1, keepdims=True) + bias, (64, 128))

    def project(s, c):
        xcopy(s).wait()
        x = xv[s]
        p = lax.dot_general(wst[...], x, (((1,), (1,)), ((), ())), preferred_element_type=F32)
        mean_rows = jnp.dot(x, jnp.ones((CH, 128), BF16), preferred_element_type=F32) * (1.0 / CH)
        xf = x.astype(F32)
        d0 = xf[:, :128] - mean_rows
        d1 = xf[:, 128:] - mean_rows
        sq = jnp.concatenate([(d0 * d0).astype(BF16), (d1 * d1).astype(BF16)], axis=1)
        v = lax.dot_general(jnp.ones((16, CH), BF16), sq, (((1,), (1,)), ((), ())), preferred_element_type=F32)
        for t in range(8):
            lanes = slice(t * 128, (t + 1) * 128)
            mean = p[128:129, lanes] * (1.0 / CH)
            scale = lax.rsqrt(v[0:1, lanes] * (1.0 / CH) + 1e-5)
            y = (p[0:64, lanes] + p[64:128, lanes] - mean * cst[0]) * scale + cst[1]
            stage[t, pl.ds(s, 64, stride=SEQS), :] = y
        return c

    lax.fori_loop(0, SEQS, project, 0)

    for t in range(8):
        mask = m_ref[:, t * 128 : (t + 1) * 128].astype(F32)
        mask2 = jnp.concatenate([mask, mask], axis=0).astype(BF16)
        for mat in range(2):
            for h in range(2):
                at = mat * 256 + h * 128
                y = stage[t, at : at + 128, :].reshape(HALF, SEQS, 128) * mask
                sbuf[mat, t * 2 + h, 0:128, :] = y.reshape(128, 128).astype(BF16)
                sbuf[mat, t * 2 + h, 128:144, :] = mask2

    pl.semaphore_wait(barrier, 29)

    def acopy(mat, p):
        return pltpu.make_async_remote_copy(
            src_ref=sbuf.at[mat, p], dst_ref=abuf.at[mat, place[mat]],
            send_sem=asend.at[mat, p], recv_sem=arecv.at[mat, place[mat]],
            device_id=exchange_id(mat, p), device_id_type=MESH)

    def aland(mat, p):
        return pltpu.make_async_remote_copy(
            src_ref=sbuf.at[mat, p], dst_ref=abuf.at[mat, p],
            send_sem=asend.at[mat, p], recv_sem=arecv.at[mat, p],
            device_id=exchange_id(mat, p), device_id_type=MESH)

    def asend_all(d, c):
        for mat in range(2):
            acopy(mat, lax.rem(place[mat] + d, 16)).start()
        return c

    lax.fori_loop(1, 16, asend_all, 0)
    for mat in range(2):
        abuf[mat, place[mat]] = sbuf[mat, place[mat]]
    acc[...] = jnp.zeros_like(acc)

    fsc[...] = f_ref[...].astype(F32)
    for g in range(GROUPS):
        parts = []
        for rh in range(2):
            for e in range(NE):
                for lh in range(2):
                    re = rh + core - 2 * rh * core
                    le = lh + core - 2 * lh * core
                    parts.append(fsc[pl.ds(le * 512 + re * HALF + (g * NE + e), HALF, stride=32), :])
        ft_ref[g] = jnp.concatenate(parts, axis=0).T.astype(BF16)

    def await_all(mat):
        def one(d, c):
            aland(mat, lax.rem(place[mat] + d, 16)).wait_recv()
            return c

        lax.fori_loop(1, 16, one, 0)

    def slot(mat, g, k):
        return lg.at[g, k] if mat == 0 else rg.at[g, :, k]

    def gcopy(mat, g, k, to, n):
        return pltpu.make_async_remote_copy(
            src_ref=slot(mat, g, k), dst_ref=slot(mat, g, k),
            send_sem=gsend.at[mat, g, n], recv_sem=grecv.at[mat, g, k],
            device_id=gather_id(mat, to), device_id_type=MESH)

    def scopy(mat, g, k):
        src = lg.at[g, k, 1] if mat == 0 else rg.at[g, :, k]
        dst = ls.at[g, k] if mat == 0 else rs.at[g, :, k]
        return pltpu.make_async_remote_copy(
            src_ref=src, dst_ref=dst,
            send_sem=ssend.at[mat, g, k], recv_sem=srecv.at[mat, g, k],
            device_id=(sibling, col), device_id_type=MESH)

    def mslot(mat, k):
        return lm.at[k] if mat == 0 else rm.at[:, k]

    def mcopy(mat, k, to):
        return pltpu.make_async_remote_copy(
            src_ref=mslot(mat, k), dst_ref=mslot(mat, k),
            send_sem=msend.at[mat, to], recv_sem=mrecv.at[mat, k],
            device_id=gather_id(mat, to), device_id_type=MESH)

    mate = tuple(k + 1 - 2 * lax.rem(k, 2) for k in own)

    def ring(k, steps):
        return lax.rem(k + 2 * steps, 8)

    def to_mate(mat, g):
        gcopy(mat, g, own[mat], mate[mat], 0).start()

    def to_ring(mat, g):
        k = own[mat]
        gcopy(mat, g, k, ring(k, 1), 1).start()
        gcopy(mat, g, k, ring(k, 3), 2).start()
        scopy(mat, g, k).start()

    def landed(mat, g, k):
        gcopy(mat, g, k, mate[mat], 0).wait_recv()

    def s1(mat, g):
        k = own[mat]
        landed(mat, g, mate[mat])
        gcopy(mat, g, mate[mat], ring(k, 1), 3).start()
        gcopy(mat, g, mate[mat], ring(k, 3), 4).start()
        scopy(mat, g, mate[mat]).start()

    def s2(mat, g):
        k = own[mat]
        landed(mat, g, ring(k, 3))
        gcopy(mat, g, ring(k, 3), ring(k, 1), 5).start()
        scopy(mat, g, ring(k, 3)).start()

    def s3(mat, g):
        k = own[mat]
        landed(mat, g, ring(mate[mat], 1))
        gcopy(mat, g, ring(mate[mat], 1), ring(k, 3), 6).start()
        scopy(mat, g, ring(mate[mat], 1)).start()
        for other in (ring(k, 1), ring(mate[mat], 3)):
            landed(mat, g, other)
            scopy(mat, g, other).start()

    def s4(mat, g):
        for k in (ring(own[mat], 2), ring(mate[mat], 2)):
            landed(mat, g, k)
            scopy(mat, g, k).start()

    def s5(mat, g):
        def one(k, c):
            scopy(mat, g, k).wait_recv()
            return c

        lax.fori_loop(0, 8, one, 0)

    await_all(1)
    for pair in range(HALF // 2 + 1):
        part = abuf[1, :, pair * 16 : pair * 16 + 16, :].astype(F32).reshape(16, 2, 8, 128)
        for q in range(2):
            e = pair * 2 + q
            tile = part[:, q].reshape(8, 16, 128).astype(BF16)
            if e < HALF:
                at = (e % NE) * 128
                rg[e // NE, :, own[1], :, at : at + 128] = tile
            elif e == HALF:
                rm[:, own[1]] = tile
    for g in range(2):
        to_mate(1, g)
        to_ring(1, g)

    await_all(0)
    for pair in range(HALF // 2 + 1):
        part = abuf[0, :, pair * 16 : pair * 16 + 16, :].astype(F32).reshape(16, 2, 8, 128)
        for q in range(2):
            c = pair * 2 + q
            if c <= HALF:
                tile = part[:, q].reshape(128, 128).T
                if c < HALF:
                    t2[pl.ds(c, 128, stride=HALF), :] = tile
                else:
                    tm[...] = tile
    for g in range(GROUPS):
        for rel in range(2):
            half = core if rel == 0 else 1 - core
            rows = pl.multiple_of((half * 64 + g * NI) * HALF, NI * HALF)
            lg[g, own[0], rel] = t2[pl.ds(rows, NI * HALF), :].astype(BF16)
    lm[own[0]] = tm[pl.ds(pl.multiple_of(core * 64, 64), 64), :].astype(BF16)
    for g in range(2):
        to_mate(0, g)
        to_ring(0, g)
    for mat in range(2):
        for g in range(2, GROUPS):
            to_mate(mat, g)

    def send_masks(d, c):
        for mat in range(2):
            mcopy(mat, own[mat], lax.rem(own[mat] + d, 8)).start()
        return c

    lax.fori_loop(1, 8, send_masks, 0)

    def block(gl, gr):
        for rh in range(2):
            rhs = (rg if rh == 0 else rs)[gr].reshape(1024, NE * 128)
            for lh in range(2):
                lhs = jnp.concatenate([lg[gl, k, 0] if lh == 0 else ls[gl, k] for k in range(8)], axis=1)
                o = jnp.dot(lhs, rhs, preferred_element_type=F32).astype(BF16)
                for e in range(NE):
                    at = ((rh * NE + e) * 2 + lh) * 16
                    for i in range(NI):
                        mid[at : at + 16, i * 128 : (i + 1) * 128] = o[i * 16 : (i + 1) * 16, e * 128 : (e + 1) * 128]
        acc[gl] += jnp.dot(ft_ref[gr], mid[...], preferred_element_type=F32)

    def ocopy(gl):
        return pltpu.make_async_copy(ob.at[gl], out_hbm.at[pl.ds(gl * NI, NI)], osem.at[gl])

    def finish(gl):
        offset = jnp.broadcast_to(column(fo_ref[...], DEPTH), (DEPTH, 128))
        for i in range(NI):
            y = acc[gl, :, i * 128 : (i + 1) * 128] * cnt[pl.ds(gl * NI + i, 1), :] + offset
            ob[gl, i] = y.T.astype(BF16)
        ocopy(gl).start()

    def serve(f, g):
        if 0 <= g < GROUPS:
            for mat in range(2):
                f(mat, g)

    def compute_right(g):
        def one(r, c):
            block(g, r)
            return c

        if 0 <= g < GROUPS:
            lax.fori_loop(0, g + 1, one, 0)

    def compute_left(g):
        def one(l, c):
            if g == GROUPS - 1:
                finish(lax.rem(l + GROUPS - 1, GROUPS))
            block(l, g)
            return c

        if 0 < g < GROUPS:
            lax.fori_loop(0, g, one, 0)

    def await_masks(d, c):
        for mat in range(2):
            k = lax.rem(own[mat] + d, 8)
            mcopy(mat, k, k).wait_recv()
        return c

    for r in range(GROUPS + 3):
        serve(s5, r - 3)
        compute_right(r - 3)
        serve(s4, r - 2)
        serve(s3, r - 1)
        serve(s1, r)
        serve(s2, r)
        serve(to_ring, r + 2)
        if r == GROUPS + 1:
            lax.fori_loop(1, 8, await_masks, 0)
            lmask = jnp.concatenate([lm[k] for k in range(8)], axis=1)
            count = jnp.dot(lmask, rm[...].reshape(1024, 128), preferred_element_type=F32)
            cnt[...] = 1.0 / (count + 0.001)
        compute_left(r - 3)
    finish(GROUPS - 2)

    def asent(d, c):
        for mat in range(2):
            acopy(mat, lax.rem(place[mat] + d, 16)).wait_send()
        return c

    def msent(d, c):
        for mat in range(2):
            mcopy(mat, own[mat], lax.rem(own[mat] + d, 8)).wait_send()
        return c

    def gsent(g, c):
        for mat in range(2):
            for n in range(7):
                gcopy(mat, g, own[mat], mate[mat], n).wait_send()
            for k in range(8):
                scopy(mat, g, k).wait_send()
        return c

    lax.fori_loop(1, 16, asent, 0)
    lax.fori_loop(1, 8, msent, 0)
    lax.fori_loop(0, GROUPS, gsent, 0)
    for gl in range(GROUPS):
        ocopy(gl).wait()


def shards(x, mask, gain, off, w1, b1, w2, b2, final, final_offset):
    vmem = pl.BlockSpec(memory_space=pltpu.VMEM)
    hbm = pl.BlockSpec(memory_space=pl.ANY)
    dma = pltpu.SemaphoreType.DMA
    return pl.pallas_call(
        kernel,
        out_shape=jax.ShapeDtypeStruct((64, 128, DEPTH), BF16),
        in_specs=[hbm] + [vmem] * 9,
        out_specs=hbm,
        scratch_shapes=[
            pltpu.VMEM((SEQS, RES, CH), BF16),
            pltpu.VMEM((144, CH), BF16),
            pltpu.VMEM((2, 64, 128), F32),
            pltpu.VMEM((1024, DEPTH), F32),
            pltpu.VMEM((GROUPS, DEPTH, 64 * NE), BF16),
            pltpu.VMEM((8, 64 * SEQS, 128), F32),
            pltpu.VMEM((2, 16, PIECE, 128), BF16),
            pltpu.VMEM((2, 16, PIECE, 128), BF16),
            pltpu.VMEM((128 * HALF, 128), F32),
            pltpu.VMEM((128, 128), F32),
            pltpu.VMEM((GROUPS, 8, 2, NI * HALF, 128), BF16),
            pltpu.VMEM((GROUPS, 8, NI * HALF, 128), BF16),
            pltpu.VMEM((GROUPS, 8, 8, 16, NE * 128), BF16),
            pltpu.VMEM((GROUPS, 8, 8, 16, NE * 128), BF16),
            pltpu.VMEM((8, 64, 128), BF16),
            pltpu.VMEM((8, 8, 16, 128), BF16),
            pltpu.VMEM((64 * NE, NI * 128), BF16),
            pltpu.VMEM((GROUPS, DEPTH, NI * 128), F32),
            pltpu.VMEM((64, 128), F32),
            pltpu.VMEM((GROUPS, NI, 128, DEPTH), BF16),
            dma((SEQS,)),
            dma((2, 16)),
            dma((2, 16)),
            dma((2, GROUPS, 8)),
            dma((2, GROUPS, 8)),
            dma((2, GROUPS, 8)),
            dma((2, GROUPS, 8)),
            dma((2, 8)),
            dma((2, 8)),
            dma((GROUPS,)),
        ],
        compiler_params=pltpu.CompilerParams(
            collective_id=0, has_side_effects=True, vmem_limit_bytes=56 * 1024 * 1024),
        cost_estimate=pl.CostEstimate(flops=20_000_000_000, bytes_accessed=8_000_000, transcendentals=0),
    )(x, mask, gain.reshape(1, CH), off.reshape(1, CH), w1.T, b1.reshape(1, 32), w2.T, b2.reshape(1, 32),
      final, final_offset.reshape(1, DEPTH))


def solution(mesh):
    every = P(("row", "col"))
    in_specs = (every, every) + (P(),) * 8
    return jax.shard_map(shards, mesh=mesh, in_specs=in_specs, out_specs=P("row", "col", None), check_vma=False)
```

```python
import jax
import jax.numpy as jnp
from jax import lax
from jax.experimental import pallas as pl
from jax.experimental.pallas import tpu as pltpu
from jax.sharding import PartitionSpec as P

F32 = jnp.float32
BF16 = jnp.bfloat16
MESH = pl.DeviceIdType.MESH

SEQS = 8
RES = 1024
CH = 256
HALF = 16
GROUPS = 4
GP = GROUPS // 2
AHEAD = 4
NI = 64 // GROUPS
NE = HALF // GROUPS
DEPTH = 128


def column(row, n):
    eye = lax.broadcasted_iota(jnp.int32, (n, n), 0) == lax.broadcasted_iota(jnp.int32, (n, n), 1)
    return jnp.sum(jnp.where(eye, jnp.broadcast_to(row, (n, n)), 0.0), axis=1, keepdims=True)


def kernel(
    x_hbm, m_ref, gain_ref, off_ref, w1_ref, b1_ref, w2_ref, b2_ref, f_ref, fo_ref,
    out_hbm,
    xv, wst, cst, fsc, ft_ref, stage, sbuf0, sbuf1, abuf0, abuf1, t2, tm, lg, rg, rs, lm, rm, mid, acc, cnt, ob,
    xsem, asend, arecv, gsend, grecv, ssend, srecv, msend, mrecv, osem,
):
    row = lax.axis_index("row")
    col = lax.axis_index("col")
    core = lax.rem(row, 2)
    sibling = row + 1 - 2 * core
    own = (col, row // 2)
    place = (row, col * 2 + core)

    def exchange_id(mat, p):
        return (p, col) if mat == 0 else ((row // 2) * 2 + lax.rem(p, 2), p // 2)

    def gather_id(mat, k):
        return (row, k) if mat == 0 else (k * 2 + core, col)

    barrier = pltpu.get_barrier_semaphore()

    def hello(d, c):
        pl.semaphore_signal(barrier, inc=1, device_id=exchange_id(0, lax.rem(row + d, 16)), device_id_type=MESH)
        return c

    def hello_cols(d, c):
        k = lax.rem(col + d, 8)
        pl.semaphore_signal(barrier, inc=1, device_id=(row, k), device_id_type=MESH)
        pl.semaphore_signal(barrier, inc=1, device_id=(sibling, k), device_id_type=MESH)
        return c

    lax.fori_loop(1, 16, hello, 0)
    lax.fori_loop(1, 8, hello_cols, 0)

    def xcopy(s):
        return pltpu.make_async_copy(x_hbm.at[s], xv.at[s], xsem.at[s])

    for s in range(SEQS):
        xcopy(s).start()

    wt = jnp.concatenate([w1_ref[...].astype(F32), w2_ref[...].astype(F32)], axis=0)
    gw = wt * gain_ref[...]
    hi = gw.astype(BF16)
    lo = (gw - hi.astype(F32)).astype(BF16)
    wst[0:64] = hi
    wst[64:128] = lo
    wst[128:144] = jnp.ones((16, CH), BF16)
    cst[0] = jnp.broadcast_to(jnp.sum(hi.astype(F32) + lo.astype(F32), axis=1, keepdims=True), (64, 128))
    bias = jnp.concatenate([column(b1_ref[...], 32), column(b2_ref[...], 32)], axis=0)
    cst[1] = jnp.broadcast_to(jnp.sum(wt * off_ref[...], axis=1, keepdims=True) + bias, (64, 128))

    def project(s, c):
        xcopy(s).wait()
        x = xv[s]
        p = lax.dot_general(wst[...], x, (((1,), (1,)), ((), ())), preferred_element_type=F32)
        mean_rows = jnp.dot(x, jnp.ones((CH, 128), BF16), preferred_element_type=F32) * (1.0 / CH)
        xf = x.astype(F32)
        d0 = xf[:, :128] - mean_rows
        d1 = xf[:, 128:] - mean_rows
        sq = jnp.concatenate([(d0 * d0).astype(BF16), (d1 * d1).astype(BF16)], axis=1)
        v = lax.dot_general(jnp.ones((16, CH), BF16), sq, (((1,), (1,)), ((), ())), preferred_element_type=F32)
        for t in range(8):
            lanes = slice(t * 128, (t + 1) * 128)
            mean = p[128:129, lanes] * (1.0 / CH)
            scale = lax.rsqrt(v[0:1, lanes] * (1.0 / CH) + 1e-5)
            y = (p[0:64, lanes] + p[64:128, lanes] - mean * cst[0]) * scale + cst[1]
            stage[t, pl.ds(s, 64, stride=SEQS), :] = y
        return c

    lax.fori_loop(0, SEQS, project, 0)

    lane = lax.broadcasted_iota(jnp.int32, (64, 128), 1) // 32
    for t in range(8):
        mask = m_ref[:, t * 128 : (t + 1) * 128].astype(F32)
        mask2 = jnp.concatenate([mask, mask], axis=0).astype(BF16)
        left = (stage[t, 0:256, :].reshape(32, SEQS, 128) * mask).reshape(8, 4, SEQS, 128)
        turned = [
            [x if k == 0 else pltpu.roll(x, 32 * k, 1) for k in range(4)]
            for x in (left[:, b].reshape(64, 128) for b in range(4))
        ]
        for h in range(2):
            right = (stage[t, 256 + h * 128 : 384 + h * 128, :].reshape(HALF, SEQS, 128) * mask).reshape(128, 128)
            for part, buf in enumerate((sbuf0, sbuf1)):
                q = h * 2 + part
                y = turned[0][(0 - q) % 4]
                for b in range(1, 4):
                    y = jnp.where(lane == b, turned[b][(b - q) % 4], y)
                buf[0, t * 2 + h, 0:64, :] = y.astype(BF16)
                buf[1, t * 2 + h, 0:64, :] = right[part * 64 : part * 64 + 64].astype(BF16)
            for mat in range(2):
                sbuf1[mat, t * 2 + h, 64:80, :] = mask2

    pl.semaphore_wait(barrier, 29)

    sbuf, abuf = (sbuf0, sbuf1), (abuf0, abuf1)

    def acopy(part, mat, p):
        return pltpu.make_async_remote_copy(
            src_ref=sbuf[part].at[mat, p], dst_ref=abuf[part].at[mat, place[mat]],
            send_sem=asend.at[part, mat, p], recv_sem=arecv.at[part, mat, place[mat]],
            device_id=exchange_id(mat, p), device_id_type=MESH)

    def aland(part, mat, p):
        return pltpu.make_async_remote_copy(
            src_ref=sbuf[part].at[mat, p], dst_ref=abuf[part].at[mat, p],
            send_sem=asend.at[part, mat, p], recv_sem=arecv.at[part, mat, p],
            device_id=exchange_id(mat, p), device_id_type=MESH)

    def exchange(part):
        def one(d, c):
            for mat in range(2):
                acopy(part, mat, lax.rem(place[mat] + d, 16)).start()
            return c

        lax.fori_loop(1, 16, one, 0)
        for mat in range(2):
            abuf[part][mat, place[mat]] = sbuf[part][mat, place[mat]]

    def exchanged(part, mat):
        def one(d, c):
            aland(part, mat, lax.rem(place[mat] + d, 16)).wait_recv()
            return c

        lax.fori_loop(1, 16, one, 0)

    exchange(0)
    exchange(1)
    acc[...] = jnp.zeros_like(acc)

    fsc[...] = f_ref[...].astype(F32)
    for g in range(GROUPS):
        parts = []
        for rh in range(2):
            re = rh + core - 2 * rh * core
            for e in range(NE):
                parts.append(fsc[pl.ds(re * HALF + (g * NE + e), 32, stride=32), :])
        ft_ref[g] = jnp.concatenate(parts, axis=0).T.astype(BF16)

    def slot(mat, g, k):
        return lg.at[g, k] if mat == 0 else rg.at[g, :, k]

    def gcopy(mat, g, k, to, n):
        return pltpu.make_async_remote_copy(
            src_ref=slot(mat, g, k), dst_ref=slot(mat, g, k),
            send_sem=gsend.at[mat, g, n], recv_sem=grecv.at[mat, g, k],
            device_id=gather_id(mat, to), device_id_type=MESH)

    def scopy(g, k):
        return pltpu.make_async_remote_copy(
            src_ref=rg.at[g, :, k], dst_ref=rs.at[g, :, k],
            send_sem=ssend.at[g, k], recv_sem=srecv.at[g, k],
            device_id=(sibling, col), device_id_type=MESH)

    def share(mat, g, k):
        if mat == 1:
            scopy(g, k).start()

    def mslot(mat, k):
        return lm.at[k] if mat == 0 else rm.at[:, k]

    def mcopy(mat, k, to):
        return pltpu.make_async_remote_copy(
            src_ref=mslot(mat, k), dst_ref=mslot(mat, k),
            send_sem=msend.at[mat, to], recv_sem=mrecv.at[mat, k],
            device_id=gather_id(mat, to), device_id_type=MESH)

    mate = tuple(k + 1 - 2 * lax.rem(k, 2) for k in own)

    def ring(k, steps):
        return lax.rem(k + 2 * steps, 8)

    def to_mate(mat, g):
        gcopy(mat, g, own[mat], mate[mat], 0).start()

    def to_ring(mat, g):
        k = own[mat]
        gcopy(mat, g, k, ring(k, 1), 1).start()
        gcopy(mat, g, k, ring(k, 3), 2).start()
        share(mat, g, k)

    def landed(mat, g, k):
        gcopy(mat, g, k, mate[mat], 0).wait_recv()

    def s1(mat, g):
        k = own[mat]
        landed(mat, g, mate[mat])
        if g + 2 < GROUPS:
            to_mate(mat, g + 2)
        gcopy(mat, g, mate[mat], ring(k, 1), 3).start()
        gcopy(mat, g, mate[mat], ring(k, 3), 4).start()
        share(mat, g, mate[mat])

    def s2(mat, g):
        k = own[mat]
        landed(mat, g, ring(k, 3))
        gcopy(mat, g, ring(k, 3), ring(k, 1), 5).start()
        share(mat, g, ring(k, 3))

    def s3(mat, g):
        k = own[mat]
        landed(mat, g, ring(mate[mat], 1))
        gcopy(mat, g, ring(mate[mat], 1), ring(k, 3), 6).start()
        share(mat, g, ring(mate[mat], 1))
        for other in (ring(k, 1), ring(mate[mat], 3)):
            landed(mat, g, other)
            share(mat, g, other)

    def s4(mat, g):
        for k in (ring(own[mat], 2), ring(mate[mat], 2)):
            landed(mat, g, k)
            share(mat, g, k)

    def s5(mat, g):
        def one(k, c):
            scopy(g, k).wait_recv()
            return c

        if mat == 1:
            lax.fori_loop(0, 8, one, 0)

    def rows_of(part, mat, at):
        return abuf[part][mat, :, at : at + 16, :].astype(F32).reshape(16, 2, 8, 128)

    def prepare_right(part):
        exchanged(part, 1)
        for pair in range(4):
            both = rows_of(part, 1, pair * 16)
            for q in range(2):
                e = part * 8 + pair * 2 + q
                at = (e % NE) * 128
                rg[e // NE, :, own[1], :, at : at + 128] = both[:, q].reshape(8, 16, 128).astype(BF16)
        if part == 1:
            rm[:, own[1]] = rows_of(part, 1, 64)[:, 0].reshape(8, 16, 128).astype(BF16)

    def prepare_left(part):
        exchanged(part, 0)
        for pair in range(4):
            both = rows_of(part, 0, pair * 16)
            for q in range(2):
                tile = both[:, q].reshape(128, 128).T
                for b in range(4):
                    t2[pl.ds((pair * 2 + q) * 4 + b, 32, stride=32), :] = tile[b * 32 : b * 32 + 32]
        for g in range(GP):
            lg[part * GP + g, own[0]] = t2[g * NI * 32 : (g + 1) * NI * 32, :].astype(BF16)
        if part == 1:
            tm[...] = rows_of(part, 0, 64)[:, 0].reshape(128, 128).T
            lm[own[0]] = tm[pl.ds(pl.multiple_of(core * 64, 64), 64), :].astype(BF16)

    def begin(mat, part):
        for g in range(part * GP, part * GP + GP):
            if g < 2:
                to_mate(mat, g)
            if g < AHEAD:
                to_ring(mat, g)

    def send_masks(d, c):
        for mat in range(2):
            mcopy(mat, own[mat], lax.rem(own[mat] + d, 8)).start()
        return c

    prepare_right(0)
    begin(1, 0)
    prepare_left(0)
    begin(0, 0)
    prepare_right(1)
    begin(1, 1)
    prepare_left(1)
    begin(0, 1)
    lax.fori_loop(1, 8, send_masks, 0)

    def block(gl, gr):
        lhs = jnp.concatenate([lg[gl, k] for k in range(8)], axis=1)
        for rh in range(2):
            rhs = (rg if rh == 0 else rs)[gr].reshape(1024, NE * 128)
            o = jnp.dot(lhs, rhs, preferred_element_type=F32).astype(BF16)
            for e in range(NE):
                at = (rh * NE + e) * 32
                for i in range(NI):
                    mid[at : at + 32, i * 128 : (i + 1) * 128] = o[i * 32 : (i + 1) * 32, e * 128 : (e + 1) * 128]
        acc[gl] += jnp.dot(ft_ref[gr], mid[...], preferred_element_type=F32)

    def ocopy(gl):
        return pltpu.make_async_copy(ob.at[gl], out_hbm.at[pl.ds(gl * NI, NI)], osem.at[gl])

    def finish(gl):
        offset = jnp.broadcast_to(column(fo_ref[...], DEPTH), (DEPTH, 128))
        for i in range(NI):
            y = acc[gl, :, i * 128 : (i + 1) * 128] * cnt[pl.ds(gl * NI + i, 1), :] + offset
            ob[gl, i] = y.T.astype(BF16)
        ocopy(gl).start()

    def serve(f, g):
        if 0 <= g < GROUPS:
            for mat in range(2):
                f(mat, g)

    def compute_right(g):
        def one(r, c):
            block(g, r)
            return c

        if 0 <= g < GROUPS:
            lax.fori_loop(0, g + 1, one, 0)

    def compute_left(g):
        def one(l, c):
            block(l, g)
            return c

        if 0 < g < GROUPS:
            lax.fori_loop(0, g, one, 0)

    def await_masks(d, c):
        for mat in range(2):
            k = lax.rem(own[mat] + d, 8)
            mcopy(mat, k, k).wait_recv()
        return c

    serve(s1, 0)
    serve(s2, 0)
    serve(s1, 1)
    serve(s3, 0)
    serve(s2, 1)
    serve(s4, 0)
    serve(s1, 2)
    serve(s2, 2)
    serve(s3, 1)
    serve(s5, 0)
    compute_right(0)
    serve(s4, 1)
    serve(s1, 3)
    serve(s2, 3)
    serve(s3, 2)
    serve(s5, 1)
    compute_right(1)
    compute_left(1)
    serve(s4, 2)
    lax.fori_loop(1, 8, await_masks, 0)
    lmask = jnp.concatenate([lm[k] for k in range(8)], axis=1)
    count = jnp.dot(lmask, rm[...].reshape(1024, 128), preferred_element_type=F32)
    cnt[...] = 1.0 / (count + 0.001)
    serve(s3, 3)
    serve(s5, 2)
    compute_right(2)
    serve(s4, 3)
    compute_left(2)
    serve(s5, 3)
    for r in range(4):
        block(3, r)
    for l in range(3):
        finish((l + 3) % 4)
        block(l, 3)
    finish(GROUPS - 2)

    def asent(d, c):
        for mat in range(2):
            for part in range(2):
                acopy(part, mat, lax.rem(place[mat] + d, 16)).wait_send()
        return c

    def msent(d, c):
        for mat in range(2):
            mcopy(mat, own[mat], lax.rem(own[mat] + d, 8)).wait_send()
        return c

    def gsent(g, c):
        for mat in range(2):
            for n in range(7):
                gcopy(mat, g, own[mat], mate[mat], n).wait_send()
        for k in range(8):
            scopy(g, k).wait_send()
        return c

    lax.fori_loop(1, 16, asent, 0)
    lax.fori_loop(1, 8, msent, 0)
    lax.fori_loop(0, GROUPS, gsent, 0)
    for gl in range(GROUPS):
        ocopy(gl).wait()


def shards(x, mask, gain, off, w1, b1, w2, b2, final, final_offset):
    vmem = pl.BlockSpec(memory_space=pltpu.VMEM)
    hbm = pl.BlockSpec(memory_space=pl.ANY)
    dma = pltpu.SemaphoreType.DMA
    return pl.pallas_call(
        kernel,
        out_shape=jax.ShapeDtypeStruct((64, 128, DEPTH), BF16),
        in_specs=[hbm] + [vmem] * 9,
        out_specs=hbm,
        scratch_shapes=[
            pltpu.VMEM((SEQS, RES, CH), BF16),
            pltpu.VMEM((144, CH), BF16),
            pltpu.VMEM((2, 64, 128), F32),
            pltpu.VMEM((1024, DEPTH), F32),
            pltpu.VMEM((GROUPS, DEPTH, 64 * NE), BF16),
            pltpu.VMEM((8, 64 * SEQS, 128), F32),
            pltpu.VMEM((2, 16, 64, 128), BF16),
            pltpu.VMEM((2, 16, 80, 128), BF16),
            pltpu.VMEM((2, 16, 64, 128), BF16),
            pltpu.VMEM((2, 16, 80, 128), BF16),
            pltpu.VMEM((32 * 32, 128), F32),
            pltpu.VMEM((128, 128), F32),
            pltpu.VMEM((GROUPS, 8, NI * 32, 128), BF16),
            pltpu.VMEM((GROUPS, 8, 8, 16, NE * 128), BF16),
            pltpu.VMEM((GROUPS, 8, 8, 16, NE * 128), BF16),
            pltpu.VMEM((8, 64, 128), BF16),
            pltpu.VMEM((8, 8, 16, 128), BF16),
            pltpu.VMEM((64 * NE, NI * 128), BF16),
            pltpu.VMEM((GROUPS, DEPTH, NI * 128), F32),
            pltpu.VMEM((64, 128), F32),
            pltpu.VMEM((GROUPS, NI, 128, DEPTH), BF16),
            dma((SEQS,)),
            dma((2, 2, 16)),
            dma((2, 2, 16)),
            dma((2, GROUPS, 8)),
            dma((2, GROUPS, 8)),
            dma((GROUPS, 8)),
            dma((GROUPS, 8)),
            dma((2, 8)),
            dma((2, 8)),
            dma((GROUPS,)),
        ],
        compiler_params=pltpu.CompilerParams(
            collective_id=0, has_side_effects=True, vmem_limit_bytes=56 * 1024 * 1024),
        cost_estimate=pl.CostEstimate(flops=20_000_000_000, bytes_accessed=8_000_000, transcendentals=0),
    )(x, mask, gain.reshape(1, CH), off.reshape(1, CH), w1.T, b1.reshape(1, 32), w2.T, b2.reshape(1, 32),
      final, final_offset.reshape(1, DEPTH))


def solution(mesh):
    every = P(("row", "col"))
    in_specs = (every, every) + (P(),) * 8
    return jax.shard_map(shards, mesh=mesh, in_specs=in_specs, out_specs=P("row", "col", None), check_vma=False)
```

```python
import jax
import jax.numpy as jnp
from jax import lax
from jax.experimental import pallas as pl
from jax.experimental.pallas import tpu as pltpu
from jax.sharding import PartitionSpec as P

F32 = jnp.float32
BF16 = jnp.bfloat16
MESH = pl.DeviceIdType.MESH

SEQS = 8
RES = 1024
CH = 256
HALF = 16
GROUPS = 4
GP = GROUPS // 2
AHEAD = 4
NI = 64 // GROUPS
NE = HALF // GROUPS
DEPTH = 128


def column(row, n):
    eye = lax.broadcasted_iota(jnp.int32, (n, n), 0) == lax.broadcasted_iota(jnp.int32, (n, n), 1)
    return jnp.sum(jnp.where(eye, jnp.broadcast_to(row, (n, n)), 0.0), axis=1, keepdims=True)


def kernel(
    x_hbm, m_ref, gain_ref, off_ref, w1_ref, b1_ref, w2_ref, b2_ref, f_ref, fo_ref,
    out_hbm,
    xv, wst, cst, fsc, ft_ref, stage, sbuf0, sbuf1, abuf0, abuf1, t2, tm, lg, rg, rs, lm, rm, mid, acc, cnt, ob,
    xsem, asend, arecv, gsend, grecv, ssend, srecv, msend, mrecv, osem,
):
    row = lax.axis_index("row")
    col = lax.axis_index("col")
    core = lax.rem(row, 2)
    sibling = row + 1 - 2 * core
    own = (col, row // 2)
    place = (row, col * 2 + core)

    def exchange_id(mat, p):
        return (p, col) if mat == 0 else ((row // 2) * 2 + lax.rem(p, 2), p // 2)

    def gather_id(mat, k):
        return (row, k) if mat == 0 else (k * 2 + core, col)

    barrier = pltpu.get_barrier_semaphore()

    def hello(d, c):
        pl.semaphore_signal(barrier, inc=1, device_id=exchange_id(0, lax.rem(row + d, 16)), device_id_type=MESH)
        return c

    def hello_cols(d, c):
        k = lax.rem(col + d, 8)
        pl.semaphore_signal(barrier, inc=1, device_id=(row, k), device_id_type=MESH)
        pl.semaphore_signal(barrier, inc=1, device_id=(sibling, k), device_id_type=MESH)
        return c

    lax.fori_loop(1, 16, hello, 0)
    lax.fori_loop(1, 8, hello_cols, 0)

    def xcopy(s):
        return pltpu.make_async_copy(x_hbm.at[s], xv.at[s], xsem.at[s])

    for s in range(SEQS):
        xcopy(s).start()

    wt = jnp.concatenate([w1_ref[...].astype(F32), w2_ref[...].astype(F32)], axis=0)
    gw = wt * gain_ref[...]
    hi = gw.astype(BF16)
    lo = (gw - hi.astype(F32)).astype(BF16)
    wst[0:64] = hi
    wst[64:128] = lo
    wst[128:144] = jnp.ones((16, CH), BF16)
    cst[0] = jnp.broadcast_to(jnp.sum(hi.astype(F32) + lo.astype(F32), axis=1, keepdims=True), (64, 128))
    bias = jnp.concatenate([column(b1_ref[...], 32), column(b2_ref[...], 32)], axis=0)
    cst[1] = jnp.broadcast_to(jnp.sum(wt * off_ref[...], axis=1, keepdims=True) + bias, (64, 128))

    def project(s, c):
        xcopy(s).wait()
        x = xv[s]
        p = lax.dot_general(wst[...], x, (((1,), (1,)), ((), ())), preferred_element_type=F32)
        mean_rows = jnp.dot(x, jnp.ones((CH, 128), BF16), preferred_element_type=F32) * (1.0 / CH)
        xf = x.astype(F32)
        d0 = xf[:, :128] - mean_rows
        d1 = xf[:, 128:] - mean_rows
        sq = jnp.concatenate([(d0 * d0).astype(BF16), (d1 * d1).astype(BF16)], axis=1)
        v = lax.dot_general(jnp.ones((16, CH), BF16), sq, (((1,), (1,)), ((), ())), preferred_element_type=F32)
        for t in range(8):
            lanes = slice(t * 128, (t + 1) * 128)
            mean = p[128:129, lanes] * (1.0 / CH)
            scale = lax.rsqrt(v[0:1, lanes] * (1.0 / CH) + 1e-5)
            y = (p[0:64, lanes] + p[64:128, lanes] - mean * cst[0]) * scale + cst[1]
            stage[t, pl.ds(s, 64, stride=SEQS), :] = y
        return c

    lax.fori_loop(0, SEQS, project, 0)

    lane = lax.broadcasted_iota(jnp.int32, (64, 128), 1) // 32
    for t in range(8):
        mask = m_ref[:, t * 128 : (t + 1) * 128].astype(F32)
        mask2 = jnp.concatenate([mask, mask], axis=0).astype(BF16)
        left = (stage[t, 0:256, :].reshape(32, SEQS, 128) * mask).reshape(8, 4, SEQS, 128)
        turned = [
            [x if k == 0 else pltpu.roll(x, 32 * k, 1) for k in range(4)]
            for x in (left[:, b].reshape(64, 128) for b in range(4))
        ]
        for h in range(2):
            right = (stage[t, 256 + h * 128 : 384 + h * 128, :].reshape(HALF, SEQS, 128) * mask).reshape(128, 128)
            for part, buf in enumerate((sbuf0, sbuf1)):
                q = h * 2 + part
                y = turned[0][(0 - q) % 4]
                for b in range(1, 4):
                    y = jnp.where(lane == b, turned[b][(b - q) % 4], y)
                buf[0, t * 2 + h, 0:64, :] = y.astype(BF16)
                buf[1, t * 2 + h, 0:64, :] = right[part * 64 : part * 64 + 64].astype(BF16)
            for mat in range(2):
                sbuf1[mat, t * 2 + h, 64:80, :] = mask2

    pl.semaphore_wait(barrier, 29)

    sbuf, abuf = (sbuf0, sbuf1), (abuf0, abuf1)

    def acopy(part, mat, p):
        return pltpu.make_async_remote_copy(
            src_ref=sbuf[part].at[mat, p], dst_ref=abuf[part].at[mat, place[mat]],
            send_sem=asend.at[part, mat, p], recv_sem=arecv.at[part, mat, place[mat]],
            device_id=exchange_id(mat, p), device_id_type=MESH)

    def aland(part, mat, p):
        return pltpu.make_async_remote_copy(
            src_ref=sbuf[part].at[mat, p], dst_ref=abuf[part].at[mat, p],
            send_sem=asend.at[part, mat, p], recv_sem=arecv.at[part, mat, p],
            device_id=exchange_id(mat, p), device_id_type=MESH)

    def exchange(part):
        def one(d, c):
            for mat in range(2):
                acopy(part, mat, lax.rem(place[mat] + d, 16)).start()
            return c

        lax.fori_loop(1, 16, one, 0)
        for mat in range(2):
            abuf[part][mat, place[mat]] = sbuf[part][mat, place[mat]]

    def exchanged(part, mat):
        def one(d, c):
            aland(part, mat, lax.rem(place[mat] + d, 16)).wait_recv()
            return c

        lax.fori_loop(1, 16, one, 0)

    exchange(0)
    exchange(1)
    acc[...] = jnp.zeros_like(acc)

    fsc[...] = f_ref[...].astype(F32)
    for g in range(GROUPS):
        parts = []
        for rh in range(2):
            re = rh + core - 2 * rh * core
            for e in range(NE):
                parts.append(fsc[pl.ds(re * HALF + (g * NE + e), 32, stride=32), :])
        ft_ref[g] = jnp.concatenate(parts, axis=0).T.astype(BF16)

    def slot(mat, g, k):
        return lg.at[g, k] if mat == 0 else rg.at[g, :, k]

    def gcopy(mat, g, k, to, n):
        return pltpu.make_async_remote_copy(
            src_ref=slot(mat, g, k), dst_ref=slot(mat, g, k),
            send_sem=gsend.at[mat, g, n], recv_sem=grecv.at[mat, g, k],
            device_id=gather_id(mat, to), device_id_type=MESH)

    def scopy(g, k):
        return pltpu.make_async_remote_copy(
            src_ref=rg.at[g, :, k], dst_ref=rs.at[g, :, k],
            send_sem=ssend.at[g, k], recv_sem=srecv.at[g, k],
            device_id=(sibling, col), device_id_type=MESH)

    def share(mat, g, k):
        if mat == 1:
            scopy(g, k).start()

    def mslot(mat, k):
        return lm.at[k] if mat == 0 else rm.at[:, k]

    def mcopy(mat, k, to):
        return pltpu.make_async_remote_copy(
            src_ref=mslot(mat, k), dst_ref=mslot(mat, k),
            send_sem=msend.at[mat, to], recv_sem=mrecv.at[mat, k],
            device_id=gather_id(mat, to), device_id_type=MESH)

    mate = tuple(k + 1 - 2 * lax.rem(k, 2) for k in own)

    def ring(k, steps):
        return lax.rem(k + 2 * steps, 8)

    def to_mate(mat, g):
        gcopy(mat, g, own[mat], mate[mat], 0).start()

    def to_ring(mat, g):
        k = own[mat]
        gcopy(mat, g, k, ring(k, 1), 1).start()
        gcopy(mat, g, k, ring(k, 3), 2).start()
        share(mat, g, k)

    def landed(mat, g, k):
        gcopy(mat, g, k, mate[mat], 0).wait_recv()

    def s1(mat, g):
        k = own[mat]
        landed(mat, g, mate[mat])
        if g + 2 < GROUPS:
            to_mate(mat, g + 2)
        gcopy(mat, g, mate[mat], ring(k, 1), 3).start()
        gcopy(mat, g, mate[mat], ring(k, 3), 4).start()
        share(mat, g, mate[mat])

    def s2(mat, g):
        k = own[mat]
        landed(mat, g, ring(k, 3))
        gcopy(mat, g, ring(k, 3), ring(k, 1), 5).start()
        share(mat, g, ring(k, 3))

    def s3(mat, g):
        k = own[mat]
        landed(mat, g, ring(mate[mat], 1))
        gcopy(mat, g, ring(mate[mat], 1), ring(k, 3), 6).start()
        share(mat, g, ring(mate[mat], 1))
        for other in (ring(k, 1), ring(mate[mat], 3)):
            landed(mat, g, other)
            share(mat, g, other)

    def s4(mat, g):
        for k in (ring(own[mat], 2), ring(mate[mat], 2)):
            landed(mat, g, k)
            share(mat, g, k)

    def s5(mat, g):
        def one(k, c):
            scopy(g, k).wait_recv()
            return c

        if mat == 1:
            lax.fori_loop(0, 8, one, 0)

    def rows_of(part, mat, at):
        return abuf[part][mat, :, at : at + 16, :].astype(F32).reshape(16, 2, 8, 128)

    def prepare_right(part):
        exchanged(part, 1)
        for pair in range(4):
            both = rows_of(part, 1, pair * 16)
            for q in range(2):
                e = part * 8 + pair * 2 + q
                at = (e % NE) * 128
                rg[e // NE, :, own[1], :, at : at + 128] = both[:, q].reshape(8, 16, 128).astype(BF16)
        if part == 1:
            rm[:, own[1]] = rows_of(part, 1, 64)[:, 0].reshape(8, 16, 128).astype(BF16)

    def prepare_left(part):
        exchanged(part, 0)
        for pair in range(4):
            both = rows_of(part, 0, pair * 16)
            for q in range(2):
                tile = both[:, q].reshape(128, 128).T
                for b in range(4):
                    t2[pl.ds((pair * 2 + q) * 4 + b, 32, stride=32), :] = tile[b * 32 : b * 32 + 32]
        for g in range(GP):
            lg[part * GP + g, own[0]] = t2[g * NI * 32 : (g + 1) * NI * 32, :].astype(BF16)
        if part == 1:
            tm[...] = rows_of(part, 0, 64)[:, 0].reshape(128, 128).T
            lm[own[0]] = tm[pl.ds(pl.multiple_of(core * 64, 64), 64), :].astype(BF16)

    def begin(mat, part):
        for g in range(part * GP, part * GP + GP):
            if g < 2:
                to_mate(mat, g)
            if g < AHEAD:
                to_ring(mat, g)

    def send_masks(d, c):
        for mat in range(2):
            mcopy(mat, own[mat], lax.rem(own[mat] + d, 8)).start()
        return c

    prepare_right(0)
    begin(1, 0)
    prepare_left(0)
    begin(0, 0)
    prepare_right(1)
    begin(1, 1)
    prepare_left(1)
    begin(0, 1)
    lax.fori_loop(1, 8, send_masks, 0)

    def block(gl, gr):
        lhs = jnp.concatenate([lg[gl, k] for k in range(8)], axis=1)
        for rh in range(2):
            rhs = (rg if rh == 0 else rs)[gr].reshape(1024, NE * 128)
            o = jnp.dot(lhs, rhs, preferred_element_type=F32).astype(BF16)
            for e in range(NE):
                at = (rh * NE + e) * 32
                for i in range(NI):
                    mid[at : at + 32, i * 128 : (i + 1) * 128] = o[i * 32 : (i + 1) * 32, e * 128 : (e + 1) * 128]
        acc[gl] += jnp.dot(ft_ref[gr], mid[...], preferred_element_type=F32)

    def ocopy(gl):
        return pltpu.make_async_copy(ob.at[gl], out_hbm.at[pl.ds(gl * NI, NI)], osem.at[gl])

    def finish(gl):
        offset = jnp.broadcast_to(column(fo_ref[...], DEPTH), (DEPTH, 128))
        for i in range(NI):
            y = acc[gl, :, i * 128 : (i + 1) * 128] * cnt[pl.ds(gl * NI + i, 1), :] + offset
            ob[gl, i] = y.T.astype(BF16)
        ocopy(gl).start()

    def serve(f, g):
        if 0 <= g < GROUPS:
            for mat in range(2):
                f(mat, g)

    def compute_right(g):
        def one(r, c):
            block(g, r)
            return c

        if 0 <= g < GROUPS:
            lax.fori_loop(0, g + 1, one, 0)

    def compute_left(g):
        def one(l, c):
            block(l, g)
            return c

        if 0 < g < GROUPS:
            lax.fori_loop(0, g, one, 0)

    def await_masks(d, c):
        for mat in range(2):
            k = lax.rem(own[mat] + d, 8)
            mcopy(mat, k, k).wait_recv()
        return c

    serve(s1, 0)
    serve(s2, 0)
    serve(s1, 1)
    serve(s3, 0)
    serve(s2, 1)
    serve(s4, 0)
    serve(s1, 2)
    serve(s2, 2)
    serve(s3, 1)
    serve(s5, 0)
    compute_right(0)
    serve(s4, 1)
    serve(s1, 3)
    serve(s2, 3)
    serve(s3, 2)
    serve(s5, 1)
    compute_right(1)
    compute_left(1)
    serve(s4, 2)
    lax.fori_loop(1, 8, await_masks, 0)
    lmask = jnp.concatenate([lm[k] for k in range(8)], axis=1)
    count = jnp.dot(lmask, rm[...].reshape(1024, 128), preferred_element_type=F32)
    cnt[...] = 1.0 / (count + 0.001)
    serve(s3, 3)
    serve(s5, 2)
    for r in range(3):
        block(2, r)
    serve(s4, 3)
    for l in range(2):
        block(l, 2)
    serve(s5, 3)
    for r in range(4):
        block(3, r)
    for l in range(3):
        finish((l + 3) % 4)
        block(l, 3)
    finish(GROUPS - 2)

    def asent(d, c):
        for mat in range(2):
            for part in range(2):
                acopy(part, mat, lax.rem(place[mat] + d, 16)).wait_send()
        return c

    def msent(d, c):
        for mat in range(2):
            mcopy(mat, own[mat], lax.rem(own[mat] + d, 8)).wait_send()
        return c

    def gsent(g, c):
        for mat in range(2):
            for n in range(7):
                gcopy(mat, g, own[mat], mate[mat], n).wait_send()
        for k in range(8):
            scopy(g, k).wait_send()
        return c

    lax.fori_loop(1, 16, asent, 0)
    lax.fori_loop(1, 8, msent, 0)
    lax.fori_loop(0, GROUPS, gsent, 0)
    for gl in range(GROUPS):
        ocopy(gl).wait()


def shards(x, mask, gain, off, w1, b1, w2, b2, final, final_offset):
    vmem = pl.BlockSpec(memory_space=pltpu.VMEM)
    hbm = pl.BlockSpec(memory_space=pl.ANY)
    dma = pltpu.SemaphoreType.DMA
    return pl.pallas_call(
        kernel,
        out_shape=jax.ShapeDtypeStruct((64, 128, DEPTH), BF16),
        in_specs=[hbm] + [vmem] * 9,
        out_specs=hbm,
        scratch_shapes=[
            pltpu.VMEM((SEQS, RES, CH), BF16),
            pltpu.VMEM((144, CH), BF16),
            pltpu.VMEM((2, 64, 128), F32),
            pltpu.VMEM((1024, DEPTH), F32),
            pltpu.VMEM((GROUPS, DEPTH, 64 * NE), BF16),
            pltpu.VMEM((8, 64 * SEQS, 128), F32),
            pltpu.VMEM((2, 16, 64, 128), BF16),
            pltpu.VMEM((2, 16, 80, 128), BF16),
            pltpu.VMEM((2, 16, 64, 128), BF16),
            pltpu.VMEM((2, 16, 80, 128), BF16),
            pltpu.VMEM((32 * 32, 128), F32),
            pltpu.VMEM((128, 128), F32),
            pltpu.VMEM((GROUPS, 8, NI * 32, 128), BF16),
            pltpu.VMEM((GROUPS, 8, 8, 16, NE * 128), BF16),
            pltpu.VMEM((GROUPS, 8, 8, 16, NE * 128), BF16),
            pltpu.VMEM((8, 64, 128), BF16),
            pltpu.VMEM((8, 8, 16, 128), BF16),
            pltpu.VMEM((64 * NE, NI * 128), BF16),
            pltpu.VMEM((GROUPS, DEPTH, NI * 128), F32),
            pltpu.VMEM((64, 128), F32),
            pltpu.VMEM((GROUPS, NI, 128, DEPTH), BF16),
            dma((SEQS,)),
            dma((2, 2, 16)),
            dma((2, 2, 16)),
            dma((2, GROUPS, 8)),
            dma((2, GROUPS, 8)),
            dma((GROUPS, 8)),
            dma((GROUPS, 8)),
            dma((2, 8)),
            dma((2, 8)),
            dma((GROUPS,)),
        ],
        compiler_params=pltpu.CompilerParams(
            collective_id=0, has_side_effects=True, vmem_limit_bytes=56 * 1024 * 1024),
        cost_estimate=pl.CostEstimate(flops=20_000_000_000, bytes_accessed=8_000_000, transcendentals=0),
    )(x, mask, gain.reshape(1, CH), off.reshape(1, CH), w1.T, b1.reshape(1, 32), w2.T, b2.reshape(1, 32),
      final, final_offset.reshape(1, DEPTH))


def solution(mesh):
    every = P(("row", "col"))
    in_specs = (every, every) + (P(),) * 8
    return jax.shard_map(shards, mesh=mesh, in_specs=in_specs, out_specs=P("row", "col", None), check_vma=False)
```

```python
import jax
import jax.numpy as jnp
from jax import lax
from jax.experimental import pallas as pl
from jax.experimental.pallas import tpu as pltpu
from jax.sharding import PartitionSpec as P

F32 = jnp.float32
BF16 = jnp.bfloat16
MESH = pl.DeviceIdType.MESH

SEQS = 8
RES = 1024
CH = 256
HALF = 16
GROUPS = 4
GP = GROUPS // 2
AHEAD = 4
NI = 64 // GROUPS
NE = HALF // GROUPS
DEPTH = 128


def column(row, n):
    eye = lax.broadcasted_iota(jnp.int32, (n, n), 0) == lax.broadcasted_iota(jnp.int32, (n, n), 1)
    return jnp.sum(jnp.where(eye, jnp.broadcast_to(row, (n, n)), 0.0), axis=1, keepdims=True)


def kernel(
    x_hbm, m_ref, gain_ref, off_ref, w1_ref, b1_ref, w2_ref, b2_ref, f_ref, fo_ref,
    out_hbm,
    xv, wst, cst, fsc, ft_ref, stage, sbuf0, sbuf1, abuf0, abuf1, t2, tm, lg, rg, rs, lm, rm, mid, acc, cnt, ob,
    xsem, asend, arecv, gsend, grecv, ssend, srecv, msend, mrecv, osem,
):
    row = lax.axis_index("row")
    col = lax.axis_index("col")
    core = lax.rem(row, 2)
    sibling = row + 1 - 2 * core
    own = (col, row // 2)
    place = (row, col * 2 + core)

    def exchange_id(mat, p):
        return (p, col) if mat == 0 else ((row // 2) * 2 + lax.rem(p, 2), p // 2)

    def gather_id(mat, k):
        return (row, k) if mat == 0 else (k * 2 + core, col)

    barrier = pltpu.get_barrier_semaphore()

    def hello(d, c):
        pl.semaphore_signal(barrier, inc=1, device_id=exchange_id(0, lax.rem(row + d, 16)), device_id_type=MESH)
        return c

    def hello_cols(d, c):
        k = lax.rem(col + d, 8)
        pl.semaphore_signal(barrier, inc=1, device_id=(row, k), device_id_type=MESH)
        pl.semaphore_signal(barrier, inc=1, device_id=(sibling, k), device_id_type=MESH)
        return c

    lax.fori_loop(1, 16, hello, 0)
    lax.fori_loop(1, 8, hello_cols, 0)

    def xcopy(s):
        return pltpu.make_async_copy(x_hbm.at[s], xv.at[s], xsem.at[s])

    for s in range(SEQS):
        xcopy(s).start()

    wt = jnp.concatenate([w1_ref[...].astype(F32), w2_ref[...].astype(F32)], axis=0)
    gw = wt * gain_ref[...]
    hi = gw.astype(BF16)
    lo = (gw - hi.astype(F32)).astype(BF16)
    wst[0:64] = hi
    wst[64:128] = lo
    wst[128:144] = jnp.ones((16, CH), BF16)
    cst[0] = jnp.broadcast_to(jnp.sum(hi.astype(F32) + lo.astype(F32), axis=1, keepdims=True), (64, 128))
    bias = jnp.concatenate([column(b1_ref[...], 32), column(b2_ref[...], 32)], axis=0)
    cst[1] = jnp.broadcast_to(jnp.sum(wt * off_ref[...], axis=1, keepdims=True) + bias, (64, 128))

    def project(s, c):
        xcopy(s).wait()
        x = xv[s]
        p = lax.dot_general(wst[...], x, (((1,), (1,)), ((), ())), preferred_element_type=F32)
        mean_rows = jnp.dot(x, jnp.ones((CH, 128), BF16), preferred_element_type=F32) * (1.0 / CH)
        xf = x.astype(F32)
        d0 = xf[:, :128] - mean_rows
        d1 = xf[:, 128:] - mean_rows
        sq = jnp.concatenate([(d0 * d0).astype(BF16), (d1 * d1).astype(BF16)], axis=1)
        v = lax.dot_general(jnp.ones((16, CH), BF16), sq, (((1,), (1,)), ((), ())), preferred_element_type=F32)
        for t in range(8):
            lanes = slice(t * 128, (t + 1) * 128)
            mean = p[128:129, lanes] * (1.0 / CH)
            scale = lax.rsqrt(v[0:1, lanes] * (1.0 / CH) + 1e-5)
            y = (p[0:64, lanes] + p[64:128, lanes] - mean * cst[0]) * scale + cst[1]
            stage[t, pl.ds(s, 64, stride=SEQS), :] = y
        return c

    lax.fori_loop(0, SEQS, project, 0)

    lane = lax.broadcasted_iota(jnp.int32, (64, 128), 1) // 32
    for t in range(8):
        mask = m_ref[:, t * 128 : (t + 1) * 128].astype(F32)
        mask2 = jnp.concatenate([mask, mask], axis=0).astype(BF16)
        left = (stage[t, 0:256, :].reshape(32, SEQS, 128) * mask).reshape(8, 4, SEQS, 128)
        turned = [
            [x if k == 0 else pltpu.roll(x, 32 * k, 1) for k in range(4)]
            for x in (left[:, b].reshape(64, 128) for b in range(4))
        ]
        for h in range(2):
            right = (stage[t, 256 + h * 128 : 384 + h * 128, :].reshape(HALF, SEQS, 128) * mask).reshape(128, 128)
            for part, buf in enumerate((sbuf0, sbuf1)):
                q = h * 2 + part
                y = turned[0][(0 - q) % 4]
                for b in range(1, 4):
                    y = jnp.where(lane == b, turned[b][(b - q) % 4], y)
                buf[0, t * 2 + h, 0:64, :] = y.astype(BF16)
                buf[1, t * 2 + h, 0:64, :] = right[part * 64 : part * 64 + 64].astype(BF16)
            for mat in range(2):
                sbuf1[mat, t * 2 + h, 64:80, :] = mask2

    pl.semaphore_wait(barrier, 29)

    sbuf, abuf = (sbuf0, sbuf1), (abuf0, abuf1)

    def acopy(part, mat, p):
        return pltpu.make_async_remote_copy(
            src_ref=sbuf[part].at[mat, p], dst_ref=abuf[part].at[mat, place[mat]],
            send_sem=asend.at[part, mat, p], recv_sem=arecv.at[part, mat, place[mat]],
            device_id=exchange_id(mat, p), device_id_type=MESH)

    def aland(part, mat, p):
        return pltpu.make_async_remote_copy(
            src_ref=sbuf[part].at[mat, p], dst_ref=abuf[part].at[mat, p],
            send_sem=asend.at[part, mat, p], recv_sem=arecv.at[part, mat, p],
            device_id=exchange_id(mat, p), device_id_type=MESH)

    def exchange(part):
        def one(d, c):
            for mat in range(2):
                acopy(part, mat, lax.rem(place[mat] + d, 16)).start()
            return c

        lax.fori_loop(1, 16, one, 0)
        for mat in range(2):
            abuf[part][mat, place[mat]] = sbuf[part][mat, place[mat]]

    def exchanged(part, mat):
        def one(d, c):
            aland(part, mat, lax.rem(place[mat] + d, 16)).wait_recv()
            return c

        lax.fori_loop(1, 16, one, 0)

    exchange(0)
    exchange(1)
    acc[...] = jnp.zeros_like(acc)

    fsc[...] = f_ref[...].astype(F32)
    for g in range(GROUPS):
        parts = []
        for rh in range(2):
            re = rh + core - 2 * rh * core
            for e in range(NE):
                parts.append(fsc[pl.ds(re * HALF + (g * NE + e), 32, stride=32), :])
        ft_ref[g] = jnp.concatenate(parts, axis=0).T.astype(BF16)

    def slot(mat, g, k):
        return lg.at[g, k] if mat == 0 else rg.at[g, :, k]

    def gcopy(mat, g, k, to, n):
        return pltpu.make_async_remote_copy(
            src_ref=slot(mat, g, k), dst_ref=slot(mat, g, k),
            send_sem=gsend.at[mat, g, n], recv_sem=grecv.at[mat, g, k],
            device_id=gather_id(mat, to), device_id_type=MESH)

    def scopy(g, k):
        return pltpu.make_async_remote_copy(
            src_ref=rg.at[g, :, k], dst_ref=rs.at[g, :, k],
            send_sem=ssend.at[g, k], recv_sem=srecv.at[g, k],
            device_id=(sibling, col), device_id_type=MESH)

    def share(mat, g, k):
        if mat == 1:
            scopy(g, k).start()

    def mslot(mat, k):
        return lm.at[k] if mat == 0 else rm.at[:, k]

    def mcopy(mat, k, to):
        return pltpu.make_async_remote_copy(
            src_ref=mslot(mat, k), dst_ref=mslot(mat, k),
            send_sem=msend.at[mat, to], recv_sem=mrecv.at[mat, k],
            device_id=gather_id(mat, to), device_id_type=MESH)

    mate = tuple(k + 1 - 2 * lax.rem(k, 2) for k in own)

    def ring(k, steps):
        return lax.rem(k + 2 * steps, 8)

    def to_mate(mat, g):
        gcopy(mat, g, own[mat], mate[mat], 0).start()

    def to_ring(mat, g):
        k = own[mat]
        gcopy(mat, g, k, ring(k, 1), 1).start()
        gcopy(mat, g, k, ring(k, 3), 2).start()
        share(mat, g, k)

    def landed(mat, g, k):
        gcopy(mat, g, k, mate[mat], 0).wait_recv()

    def s1(mat, g):
        k = own[mat]
        landed(mat, g, mate[mat])
        if g + 2 < GROUPS:
            to_mate(mat, g + 2)
        gcopy(mat, g, mate[mat], ring(k, 1), 3).start()
        gcopy(mat, g, mate[mat], ring(k, 3), 4).start()
        share(mat, g, mate[mat])

    def s2(mat, g):
        k = own[mat]
        landed(mat, g, ring(k, 3))
        gcopy(mat, g, ring(k, 3), ring(k, 1), 5).start()
        share(mat, g, ring(k, 3))

    def s3(mat, g):
        k = own[mat]
        landed(mat, g, ring(mate[mat], 1))
        gcopy(mat, g, ring(mate[mat], 1), ring(k, 3), 6).start()
        share(mat, g, ring(mate[mat], 1))
        for other in (ring(k, 1), ring(mate[mat], 3)):
            landed(mat, g, other)
            share(mat, g, other)

    def s4(mat, g):
        for k in (ring(own[mat], 2), ring(mate[mat], 2)):
            landed(mat, g, k)
            share(mat, g, k)

    def s5(mat, g):
        def one(k, c):
            scopy(g, k).wait_recv()
            return c

        if mat == 1:
            lax.fori_loop(0, 8, one, 0)

    def rows_of(part, mat, at):
        return abuf[part][mat, :, at : at + 16, :].astype(F32).reshape(16, 2, 8, 128)

    def prepare_right(part):
        exchanged(part, 1)
        for pair in range(4):
            both = rows_of(part, 1, pair * 16)
            for q in range(2):
                e = part * 8 + pair * 2 + q
                at = (e % NE) * 128
                rg[e // NE, :, own[1], :, at : at + 128] = both[:, q].reshape(8, 16, 128).astype(BF16)
        if part == 1:
            rm[:, own[1]] = rows_of(part, 1, 64)[:, 0].reshape(8, 16, 128).astype(BF16)

    def prepare_left(part):
        exchanged(part, 0)
        for pair in range(4):
            both = rows_of(part, 0, pair * 16)
            for q in range(2):
                tile = both[:, q].reshape(128, 128).T
                for b in range(4):
                    t2[pl.ds((pair * 2 + q) * 4 + b, 32, stride=32), :] = tile[b * 32 : b * 32 + 32]
        for g in range(GP):
            lg[part * GP + g, own[0]] = t2[g * NI * 32 : (g + 1) * NI * 32, :].astype(BF16)
        if part == 1:
            tm[...] = rows_of(part, 0, 64)[:, 0].reshape(128, 128).T
            lm[own[0]] = tm[pl.ds(pl.multiple_of(core * 64, 64), 64), :].astype(BF16)

    def begin(mat, part):
        for g in range(part * GP, part * GP + GP):
            if g < 2:
                to_mate(mat, g)
            if g < AHEAD:
                to_ring(mat, g)

    def send_masks(d, c):
        for mat in range(2):
            mcopy(mat, own[mat], lax.rem(own[mat] + d, 8)).start()
        return c

    prepare_right(0)
    begin(1, 0)
    prepare_left(0)
    begin(0, 0)
    prepare_right(1)
    begin(1, 1)
    prepare_left(1)
    begin(0, 1)
    lax.fori_loop(1, 8, send_masks, 0)

    def block(gl, gr):
        lhs = jnp.concatenate([lg[gl, k] for k in range(8)], axis=1)
        for rh in range(2):
            rhs = (rg if rh == 0 else rs)[gr].reshape(1024, NE * 128)
            o = jnp.dot(lhs, rhs, preferred_element_type=F32).astype(BF16)
            for e in range(NE):
                at = (rh * NE + e) * 32
                for i in range(NI):
                    mid[at : at + 32, i * 128 : (i + 1) * 128] = o[i * 32 : (i + 1) * 32, e * 128 : (e + 1) * 128]
        acc[gl] += jnp.dot(ft_ref[gr], mid[...], preferred_element_type=F32)

    def ocopy(gl):
        return pltpu.make_async_copy(ob.at[gl], out_hbm.at[pl.ds(gl * NI, NI)], osem.at[gl])

    def finish(gl):
        offset = jnp.broadcast_to(column(fo_ref[...], DEPTH), (DEPTH, 128))
        for i in range(NI):
            y = acc[gl, :, i * 128 : (i + 1) * 128] * cnt[pl.ds(gl * NI + i, 1), :] + offset
            ob[gl, i] = y.T.astype(BF16)
        ocopy(gl).start()

    def serve(f, g):
        if 0 <= g < GROUPS:
            for mat in range(2):
                f(mat, g)

    def compute_right(g):
        def one(r, c):
            block(g, r)
            return c

        if 0 <= g < GROUPS:
            lax.fori_loop(0, g + 1, one, 0)

    def compute_left(g):
        def one(l, c):
            block(l, g)
            return c

        if 0 < g < GROUPS:
            lax.fori_loop(0, g, one, 0)

    def await_masks(d, c):
        for mat in range(2):
            k = lax.rem(own[mat] + d, 8)
            mcopy(mat, k, k).wait_recv()
        return c

    serve(s1, 0)
    serve(s2, 0)
    serve(s1, 1)
    serve(s3, 0)
    serve(s2, 1)
    serve(s4, 0)
    serve(s1, 2)
    serve(s2, 2)
    serve(s3, 1)
    serve(s5, 0)
    compute_right(0)
    serve(s4, 1)
    serve(s1, 3)
    serve(s2, 3)
    serve(s3, 2)
    serve(s5, 1)
    compute_right(1)
    compute_left(1)
    serve(s4, 2)
    lax.fori_loop(1, 8, await_masks, 0)
    lmask = jnp.concatenate([lm[k] for k in range(8)], axis=1)
    count = jnp.dot(lmask, rm[...].reshape(1024, 128), preferred_element_type=F32)
    cnt[...] = 1.0 / (count + 0.001)
    serve(s3, 3)
    block(2, 0)
    block(2, 1)
    serve(s5, 2)
    block(2, 2)
    serve(s4, 3)
    for l in range(2):
        block(l, 2)
    for r in range(3):
        block(3, r)
    serve(s5, 3)
    block(3, 3)
    for l in range(3):
        finish((l + 3) % 4)
        block(l, 3)
    finish(GROUPS - 2)

    def asent(d, c):
        for mat in range(2):
            for part in range(2):
                acopy(part, mat, lax.rem(place[mat] + d, 16)).wait_send()
        return c

    def msent(d, c):
        for mat in range(2):
            mcopy(mat, own[mat], lax.rem(own[mat] + d, 8)).wait_send()
        return c

    def gsent(g, c):
        for mat in range(2):
            for n in range(7):
                gcopy(mat, g, own[mat], mate[mat], n).wait_send()
        for k in range(8):
            scopy(g, k).wait_send()
        return c

    lax.fori_loop(1, 16, asent, 0)
    lax.fori_loop(1, 8, msent, 0)
    lax.fori_loop(0, GROUPS, gsent, 0)
    for gl in range(GROUPS):
        ocopy(gl).wait()


def shards(x, mask, gain, off, w1, b1, w2, b2, final, final_offset):
    vmem = pl.BlockSpec(memory_space=pltpu.VMEM)
    hbm = pl.BlockSpec(memory_space=pl.ANY)
    dma = pltpu.SemaphoreType.DMA
    return pl.pallas_call(
        kernel,
        out_shape=jax.ShapeDtypeStruct((64, 128, DEPTH), BF16),
        in_specs=[hbm] + [vmem] * 9,
        out_specs=hbm,
        scratch_shapes=[
            pltpu.VMEM((SEQS, RES, CH), BF16),
            pltpu.VMEM((144, CH), BF16),
            pltpu.VMEM((2, 64, 128), F32),
            pltpu.VMEM((1024, DEPTH), F32),
            pltpu.VMEM((GROUPS, DEPTH, 64 * NE), BF16),
            pltpu.VMEM((8, 64 * SEQS, 128), F32),
            pltpu.VMEM((2, 16, 64, 128), BF16),
            pltpu.VMEM((2, 16, 80, 128), BF16),
            pltpu.VMEM((2, 16, 64, 128), BF16),
            pltpu.VMEM((2, 16, 80, 128), BF16),
            pltpu.VMEM((32 * 32, 128), F32),
            pltpu.VMEM((128, 128), F32),
            pltpu.VMEM((GROUPS, 8, NI * 32, 128), BF16),
            pltpu.VMEM((GROUPS, 8, 8, 16, NE * 128), BF16),
            pltpu.VMEM((GROUPS, 8, 8, 16, NE * 128), BF16),
            pltpu.VMEM((8, 64, 128), BF16),
            pltpu.VMEM((8, 8, 16, 128), BF16),
            pltpu.VMEM((64 * NE, NI * 128), BF16),
            pltpu.VMEM((GROUPS, DEPTH, NI * 128), F32),
            pltpu.VMEM((64, 128), F32),
            pltpu.VMEM((GROUPS, NI, 128, DEPTH), BF16),
            dma((SEQS,)),
            dma((2, 2, 16)),
            dma((2, 2, 16)),
            dma((2, GROUPS, 8)),
            dma((2, GROUPS, 8)),
            dma((GROUPS, 8)),
            dma((GROUPS, 8)),
            dma((2, 8)),
            dma((2, 8)),
            dma((GROUPS,)),
        ],
        compiler_params=pltpu.CompilerParams(
            collective_id=0, has_side_effects=True, vmem_limit_bytes=56 * 1024 * 1024),
        cost_estimate=pl.CostEstimate(flops=20_000_000_000, bytes_accessed=8_000_000, transcendentals=0),
    )(x, mask, gain.reshape(1, CH), off.reshape(1, CH), w1.T, b1.reshape(1, 32), w2.T, b2.reshape(1, 32),
      final, final_offset.reshape(1, DEPTH))


def solution(mesh):
    every = P(("row", "col"))
    in_specs = (every, every) + (P(),) * 8
    return jax.shard_map(shards, mesh=mesh, in_specs=in_specs, out_specs=P("row", "col", None), check_vma=False)
```

```python
import jax
import jax.numpy as jnp
from jax import lax
from jax.experimental import pallas as pl
from jax.experimental.pallas import tpu as pltpu
from jax.sharding import PartitionSpec as P

F32 = jnp.float32
BF16 = jnp.bfloat16
MESH = pl.DeviceIdType.MESH

SEQS = 8
RES = 1024
CH = 256
HALF = 16
GROUPS = 4
GP = GROUPS // 2
AHEAD = 4
NI = 64 // GROUPS
NE = HALF // GROUPS
DEPTH = 128


def column(row, n):
    eye = lax.broadcasted_iota(jnp.int32, (n, n), 0) == lax.broadcasted_iota(jnp.int32, (n, n), 1)
    return jnp.sum(jnp.where(eye, jnp.broadcast_to(row, (n, n)), 0.0), axis=1, keepdims=True)


def kernel(
    x_hbm, m_ref, gain_ref, off_ref, w1_ref, b1_ref, w2_ref, b2_ref, f_ref, fo_ref,
    out_hbm,
    xv, wst, cst, fsc, ft_ref, stage, sbuf0, sbuf1, abuf0, abuf1, t2, tm, lg, rg, rs, lm, rm, mid, acc, cnt, ob,
    xsem, asend, arecv, gsend, grecv, ssend, srecv, msend, mrecv, osem,
):
    row = lax.axis_index("row")
    col = lax.axis_index("col")
    core = lax.rem(row, 2)
    sibling = row + 1 - 2 * core
    own = (col, row // 2)
    place = (row, col * 2 + core)

    def exchange_id(mat, p):
        return (p, col) if mat == 0 else ((row // 2) * 2 + lax.rem(p, 2), p // 2)

    def gather_id(mat, k):
        return (row, k) if mat == 0 else (k * 2 + core, col)

    barrier = pltpu.get_barrier_semaphore()

    def hello(d, c):
        pl.semaphore_signal(barrier, inc=1, device_id=exchange_id(0, lax.rem(row + d, 16)), device_id_type=MESH)
        return c

    def hello_cols(d, c):
        k = lax.rem(col + d, 8)
        pl.semaphore_signal(barrier, inc=1, device_id=(row, k), device_id_type=MESH)
        pl.semaphore_signal(barrier, inc=1, device_id=(sibling, k), device_id_type=MESH)
        return c

    lax.fori_loop(1, 16, hello, 0)
    lax.fori_loop(1, 8, hello_cols, 0)

    def xcopy(s):
        return pltpu.make_async_copy(x_hbm.at[s], xv.at[s], xsem.at[s])

    for s in range(SEQS):
        xcopy(s).start()

    wt = jnp.concatenate([w1_ref[...].astype(F32), w2_ref[...].astype(F32)], axis=0)
    gw = wt * gain_ref[...]
    hi = gw.astype(BF16)
    lo = (gw - hi.astype(F32)).astype(BF16)
    wst[0:64] = hi
    wst[64:128] = lo
    wst[128:144] = jnp.ones((16, CH), BF16)
    cst[0] = jnp.broadcast_to(jnp.sum(hi.astype(F32) + lo.astype(F32), axis=1, keepdims=True), (64, 128))
    bias = jnp.concatenate([column(b1_ref[...], 32), column(b2_ref[...], 32)], axis=0)
    cst[1] = jnp.broadcast_to(jnp.sum(wt * off_ref[...], axis=1, keepdims=True) + bias, (64, 128))

    def project(s, c):
        xcopy(s).wait()
        x = xv[s]
        p = lax.dot_general(wst[...], x, (((1,), (1,)), ((), ())), preferred_element_type=F32)
        mean_rows = jnp.dot(x, jnp.ones((CH, 128), BF16), preferred_element_type=F32) * (1.0 / CH)
        xf = x.astype(F32)
        d0 = xf[:, :128] - mean_rows
        d1 = xf[:, 128:] - mean_rows
        sq = jnp.concatenate([(d0 * d0).astype(BF16), (d1 * d1).astype(BF16)], axis=1)
        v = lax.dot_general(jnp.ones((16, CH), BF16), sq, (((1,), (1,)), ((), ())), preferred_element_type=F32)
        for t in range(8):
            lanes = slice(t * 128, (t + 1) * 128)
            mean = p[128:129, lanes] * (1.0 / CH)
            scale = lax.rsqrt(v[0:1, lanes] * (1.0 / CH) + 1e-5)
            y = (p[0:64, lanes] + p[64:128, lanes] - mean * cst[0]) * scale + cst[1]
            stage[t, pl.ds(s, 64, stride=SEQS), :] = y
        return c

    lax.fori_loop(0, SEQS, project, 0)

    lane = lax.broadcasted_iota(jnp.int32, (64, 128), 1) // 32
    for t in range(8):
        mask = m_ref[:, t * 128 : (t + 1) * 128].astype(F32)
        mask2 = jnp.concatenate([mask, mask], axis=0).astype(BF16)
        left = (stage[t, 0:256, :].reshape(32, SEQS, 128) * mask).reshape(8, 4, SEQS, 128)
        turned = [
            [x if k == 0 else pltpu.roll(x, 32 * k, 1) for k in range(4)]
            for x in (left[:, b].reshape(64, 128) for b in range(4))
        ]
        for h in range(2):
            right = (stage[t, 256 + h * 128 : 384 + h * 128, :].reshape(HALF, SEQS, 128) * mask).reshape(128, 128)
            for part, buf in enumerate((sbuf0, sbuf1)):
                q = h * 2 + part
                y = turned[0][(0 - q) % 4]
                for b in range(1, 4):
                    y = jnp.where(lane == b, turned[b][(b - q) % 4], y)
                buf[0, t * 2 + h, 0:64, :] = y.astype(BF16)
                buf[1, t * 2 + h, 0:64, :] = right[part * 64 : part * 64 + 64].astype(BF16)
            for mat in range(2):
                sbuf1[mat, t * 2 + h, 64:80, :] = mask2

    pl.semaphore_wait(barrier, 29)

    sbuf, abuf = (sbuf0, sbuf1), (abuf0, abuf1)

    def acopy(part, mat, p):
        return pltpu.make_async_remote_copy(
            src_ref=sbuf[part].at[mat, p], dst_ref=abuf[part].at[mat, place[mat]],
            send_sem=asend.at[part, mat, p], recv_sem=arecv.at[part, mat, place[mat]],
            device_id=exchange_id(mat, p), device_id_type=MESH)

    def aland(part, mat, p):
        return pltpu.make_async_remote_copy(
            src_ref=sbuf[part].at[mat, p], dst_ref=abuf[part].at[mat, p],
            send_sem=asend.at[part, mat, p], recv_sem=arecv.at[part, mat, p],
            device_id=exchange_id(mat, p), device_id_type=MESH)

    def exchange(part):
        def one(d, c):
            for mat in range(2):
                acopy(part, mat, lax.rem(place[mat] + d, 16)).start()
            return c

        lax.fori_loop(1, 16, one, 0)
        for mat in range(2):
            abuf[part][mat, place[mat]] = sbuf[part][mat, place[mat]]

    def exchanged(part, mat):
        def one(d, c):
            aland(part, mat, lax.rem(place[mat] + d, 16)).wait_recv()
            return c

        lax.fori_loop(1, 16, one, 0)

    exchange(0)
    exchange(1)
    acc[...] = jnp.zeros_like(acc)

    fsc[...] = f_ref[...].astype(F32)
    for g in range(GROUPS):
        parts = []
        for rh in range(2):
            re = rh + core - 2 * rh * core
            for e in range(NE):
                parts.append(fsc[pl.ds(re * HALF + (g * NE + e), 32, stride=32), :])
        ft_ref[g] = jnp.concatenate(parts, axis=0).T.astype(BF16)

    def slot(mat, g, k):
        return lg.at[g, k] if mat == 0 else rg.at[g, :, k]

    def gcopy(mat, g, k, to, n):
        return pltpu.make_async_remote_copy(
            src_ref=slot(mat, g, k), dst_ref=slot(mat, g, k),
            send_sem=gsend.at[mat, g, n], recv_sem=grecv.at[mat, g, k],
            device_id=gather_id(mat, to), device_id_type=MESH)

    def scopy(g, k):
        return pltpu.make_async_remote_copy(
            src_ref=rg.at[g, :, k], dst_ref=rs.at[g, :, k],
            send_sem=ssend.at[g, k], recv_sem=srecv.at[g, k],
            device_id=(sibling, col), device_id_type=MESH)

    def share(mat, g, k):
        if mat == 1:
            scopy(g, k).start()

    def mslot(mat, k):
        return lm.at[k] if mat == 0 else rm.at[:, k]

    def mcopy(mat, k, to):
        return pltpu.make_async_remote_copy(
            src_ref=mslot(mat, k), dst_ref=mslot(mat, k),
            send_sem=msend.at[mat, to], recv_sem=mrecv.at[mat, k],
            device_id=gather_id(mat, to), device_id_type=MESH)

    mate = tuple(k + 1 - 2 * lax.rem(k, 2) for k in own)

    def ring(k, steps):
        return lax.rem(k + 2 * steps, 8)

    def to_mate(mat, g):
        gcopy(mat, g, own[mat], mate[mat], 0).start()

    def to_ring(mat, g):
        k = own[mat]
        gcopy(mat, g, k, ring(k, 1), 1).start()
        gcopy(mat, g, k, ring(k, 3), 2).start()
        share(mat, g, k)

    def landed(mat, g, k):
        gcopy(mat, g, k, mate[mat], 0).wait_recv()

    def s1(mat, g):
        k = own[mat]
        landed(mat, g, mate[mat])
        if g + 2 < GROUPS:
            to_mate(mat, g + 2)
        gcopy(mat, g, mate[mat], ring(k, 1), 3).start()
        gcopy(mat, g, mate[mat], ring(k, 3), 4).start()
        share(mat, g, mate[mat])

    def s2(mat, g):
        k = own[mat]
        landed(mat, g, ring(k, 3))
        gcopy(mat, g, ring(k, 3), ring(k, 1), 5).start()
        share(mat, g, ring(k, 3))

    def s3(mat, g):
        k = own[mat]
        landed(mat, g, ring(mate[mat], 1))
        gcopy(mat, g, ring(mate[mat], 1), ring(k, 3), 6).start()
        share(mat, g, ring(mate[mat], 1))
        for other in (ring(k, 1), ring(mate[mat], 3)):
            landed(mat, g, other)
            share(mat, g, other)

    def s4(mat, g):
        for k in (ring(own[mat], 2), ring(mate[mat], 2)):
            landed(mat, g, k)
            share(mat, g, k)

    def s5(mat, g):
        def one(k, c):
            scopy(g, k).wait_recv()
            return c

        if mat == 1:
            lax.fori_loop(0, 8, one, 0)

    def rows_of(part, mat, at):
        return abuf[part][mat, :, at : at + 16, :].astype(F32).reshape(16, 2, 8, 128)

    def prepare_right(part):
        exchanged(part, 1)
        for pair in range(4):
            both = rows_of(part, 1, pair * 16)
            for q in range(2):
                e = part * 8 + pair * 2 + q
                at = (e % NE) * 128
                rg[e // NE, :, own[1], :, at : at + 128] = both[:, q].reshape(8, 16, 128).astype(BF16)
        if part == 1:
            rm[:, own[1]] = rows_of(part, 1, 64)[:, 0].reshape(8, 16, 128).astype(BF16)

    def prepare_left(part):
        exchanged(part, 0)
        for pair in range(4):
            both = rows_of(part, 0, pair * 16)
            for q in range(2):
                tile = both[:, q].reshape(128, 128).T
                for b in range(4):
                    t2[pl.ds((pair * 2 + q) * 4 + b, 32, stride=32), :] = tile[b * 32 : b * 32 + 32]
        for g in range(GP):
            lg[part * GP + g, own[0]] = t2[g * NI * 32 : (g + 1) * NI * 32, :].astype(BF16)
        if part == 1:
            tm[...] = rows_of(part, 0, 64)[:, 0].reshape(128, 128).T
            lm[own[0]] = tm[pl.ds(pl.multiple_of(core * 64, 64), 64), :].astype(BF16)

    def begin(mat, part):
        for g in range(part * GP, part * GP + GP):
            if g < 2:
                to_mate(mat, g)
            if g < AHEAD:
                to_ring(mat, g)

    def send_masks(d, c):
        for mat in range(2):
            mcopy(mat, own[mat], lax.rem(own[mat] + d, 8)).start()
        return c

    prepare_right(0)
    begin(1, 0)
    prepare_left(0)
    begin(0, 0)
    prepare_right(1)
    begin(1, 1)
    prepare_left(1)
    begin(0, 1)
    lax.fori_loop(1, 8, send_masks, 0)

    def block(gl, gr):
        lhs = jnp.concatenate([lg[gl, k] for k in range(8)], axis=1)
        for rh in range(2):
            rhs = (rg if rh == 0 else rs)[gr].reshape(1024, NE * 128)
            o = jnp.dot(lhs, rhs, preferred_element_type=F32).astype(BF16)
            for e in range(NE):
                at = (rh * NE + e) * 32
                for i in range(NI):
                    mid[at : at + 32, i * 128 : (i + 1) * 128] = o[i * 32 : (i + 1) * 32, e * 128 : (e + 1) * 128]
        acc[gl] += jnp.dot(ft_ref[gr], mid[...], preferred_element_type=F32)

    def ocopy(gl):
        return pltpu.make_async_copy(ob.at[gl], out_hbm.at[pl.ds(gl * NI, NI)], osem.at[gl])

    def finish(gl):
        offset = jnp.broadcast_to(column(fo_ref[...], DEPTH), (DEPTH, 128))
        for i in range(NI):
            y = acc[gl, :, i * 128 : (i + 1) * 128] * cnt[pl.ds(gl * NI + i, 1), :] + offset
            ob[gl, i] = y.T.astype(BF16)
        ocopy(gl).start()

    def serve(f, g):
        if 0 <= g < GROUPS:
            for mat in range(2):
                f(mat, g)

    def compute_right(g):
        def one(r, c):
            block(g, r)
            return c

        if 0 <= g < GROUPS:
            lax.fori_loop(0, g + 1, one, 0)

    def compute_left(g):
        def one(l, c):
            block(l, g)
            return c

        if 0 < g < GROUPS:
            lax.fori_loop(0, g, one, 0)

    def await_masks(d, c):
        for mat in range(2):
            k = lax.rem(own[mat] + d, 8)
            mcopy(mat, k, k).wait_recv()
        return c

    serve(s1, 0)
    serve(s2, 0)
    serve(s1, 1)
    serve(s3, 0)
    serve(s2, 1)
    serve(s4, 0)
    serve(s1, 2)
    serve(s2, 2)
    serve(s3, 1)
    serve(s5, 0)
    compute_right(0)
    serve(s4, 1)
    serve(s1, 3)
    serve(s2, 3)
    serve(s3, 2)
    block(1, 0)
    serve(s5, 1)
    block(1, 1)
    block(0, 1)
    serve(s4, 2)
    lax.fori_loop(1, 8, await_masks, 0)
    lmask = jnp.concatenate([lm[k] for k in range(8)], axis=1)
    count = jnp.dot(lmask, rm[...].reshape(1024, 128), preferred_element_type=F32)
    cnt[...] = 1.0 / (count + 0.001)
    serve(s3, 3)
    block(2, 0)
    block(2, 1)
    serve(s5, 2)
    block(2, 2)
    serve(s4, 3)
    for l in range(2):
        block(l, 2)
    for r in range(3):
        block(3, r)
    serve(s5, 3)
    block(3, 3)
    for l in range(3):
        finish((l + 3) % 4)
        block(l, 3)
    finish(GROUPS - 2)

    def asent(d, c):
        for mat in range(2):
            for part in range(2):
                acopy(part, mat, lax.rem(place[mat] + d, 16)).wait_send()
        return c

    def msent(d, c):
        for mat in range(2):
            mcopy(mat, own[mat], lax.rem(own[mat] + d, 8)).wait_send()
        return c

    def gsent(g, c):
        for mat in range(2):
            for n in range(7):
                gcopy(mat, g, own[mat], mate[mat], n).wait_send()
        for k in range(8):
            scopy(g, k).wait_send()
        return c

    lax.fori_loop(1, 16, asent, 0)
    lax.fori_loop(1, 8, msent, 0)
    lax.fori_loop(0, GROUPS, gsent, 0)
    for gl in range(GROUPS):
        ocopy(gl).wait()


def shards(x, mask, gain, off, w1, b1, w2, b2, final, final_offset):
    vmem = pl.BlockSpec(memory_space=pltpu.VMEM)
    hbm = pl.BlockSpec(memory_space=pl.ANY)
    dma = pltpu.SemaphoreType.DMA
    return pl.pallas_call(
        kernel,
        out_shape=jax.ShapeDtypeStruct((64, 128, DEPTH), BF16),
        in_specs=[hbm] + [vmem] * 9,
        out_specs=hbm,
        scratch_shapes=[
            pltpu.VMEM((SEQS, RES, CH), BF16),
            pltpu.VMEM((144, CH), BF16),
            pltpu.VMEM((2, 64, 128), F32),
            pltpu.VMEM((1024, DEPTH), F32),
            pltpu.VMEM((GROUPS, DEPTH, 64 * NE), BF16),
            pltpu.VMEM((8, 64 * SEQS, 128), F32),
            pltpu.VMEM((2, 16, 64, 128), BF16),
            pltpu.VMEM((2, 16, 80, 128), BF16),
            pltpu.VMEM((2, 16, 64, 128), BF16),
            pltpu.VMEM((2, 16, 80, 128), BF16),
            pltpu.VMEM((32 * 32, 128), F32),
            pltpu.VMEM((128, 128), F32),
            pltpu.VMEM((GROUPS, 8, NI * 32, 128), BF16),
            pltpu.VMEM((GROUPS, 8, 8, 16, NE * 128), BF16),
            pltpu.VMEM((GROUPS, 8, 8, 16, NE * 128), BF16),
            pltpu.VMEM((8, 64, 128), BF16),
            pltpu.VMEM((8, 8, 16, 128), BF16),
            pltpu.VMEM((64 * NE, NI * 128), BF16),
            pltpu.VMEM((GROUPS, DEPTH, NI * 128), F32),
            pltpu.VMEM((64, 128), F32),
            pltpu.VMEM((GROUPS, NI, 128, DEPTH), BF16),
            dma((SEQS,)),
            dma((2, 2, 16)),
            dma((2, 2, 16)),
            dma((2, GROUPS, 8)),
            dma((2, GROUPS, 8)),
            dma((GROUPS, 8)),
            dma((GROUPS, 8)),
            dma((2, 8)),
            dma((2, 8)),
            dma((GROUPS,)),
        ],
        compiler_params=pltpu.CompilerParams(
            collective_id=0, has_side_effects=True, vmem_limit_bytes=56 * 1024 * 1024),
        cost_estimate=pl.CostEstimate(flops=20_000_000_000, bytes_accessed=8_000_000, transcendentals=0),
    )(x, mask, gain.reshape(1, CH), off.reshape(1, CH), w1.T, b1.reshape(1, 32), w2.T, b2.reshape(1, 32),
      final, final_offset.reshape(1, DEPTH))


def solution(mesh):
    every = P(("row", "col"))
    in_specs = (every, every) + (P(),) * 8
    return jax.shard_map(shards, mesh=mesh, in_specs=in_specs, out_specs=P("row", "col", None), check_vma=False)
```
